128 devices in a mesh: slab: 16 (over x, z), sub: 8 (over y, core).
Axes of the slice: x: 4, y: 4, z: 4, core: 2. Of those that a mesh axis runs over, the one named last changes fastest.
Arguments:
- multipoles: bfloat16 [4096, 64, 512], P(('slab', 'sub')), may hold values from -6 to 6
- translations: bfloat16 [24, 512, 512], replicated, may hold values from -0.0546875 to 0.0546875
- local_source: int32 [16, 4096], P(None, ('slab', 'sub')), may hold values from 0 to 31
- remote_owner: int32 [32768, 1], P(('slab', 'sub')), may hold values from 0 to 127; in each aligned block of 256 rows (0 to 255, 256 to 511, ...) at most 2 rows name the same one
- remote_box: int32 [32768], P(('slab', 'sub')), may hold values from 0 to 31
- charges: bfloat16 [64, 262144], P(None, ('slab', 'sub')), may hold values from -6 to 6
- positions: float32 [3, 262144], P(None, ('slab', 'sub')), may hold values from -1 to 1
- leaf_count: int32 [4096], P(('slab', 'sub')), may hold values from 1 to 64
Outputs:
- expansion: float32 [4096, 64, 512], P(('slab', 'sub'))
- potential: float32 [64, 262144], P(None, ('slab', 'sub'))
The draws below stay inside these ranges and needn't reach their ends.
Inputs may be any that keep to these rules, and one draw needn't show every extreme that they name: `remote_owner`: within the rows of one device, each source device number appears at most 2 times.
All inputs are finite; a program needn't handle non-finite values.
Results may differ from the reference program's by a relative error of at most 0.0003.
Values may be sent and summed in bfloat16 or wider, within the bound.
A program may use at most 256 MiB of HBM per device.

```python
import math
import jax
import jax.numpy as jnp
import numpy as np
from jax import lax

ORDER = 8
COEFS = 512
RHS = 64
BOX_DEV = 32
SLOTS = 64
LOCAL_TYPES = 16
REMOTE_TYPES = 8
TYPES = 24
REM_TASKS = 256
CAP = 2
BOXES = 4096
POINTS = 262144
DEVICES = 128


def plant(array, own_key, low, high):
    place = [jax.random.randint(jax.random.fold_in(own_key, axis), (), 0, length) for axis, length in enumerate(array.shape)]
    longest = array.shape.index(max(array.shape))
    next_to = place[:longest] + [(place[longest] + 1) % array.shape[longest]] + place[longest + 1:]
    return array.at[tuple(place)].set(low).at[tuple(next_to)].set(high)


def levels(own_key, shape, pieces, smallest, largest):
    def one(axis_at, blocks):
        steps = jax.random.uniform(jax.random.fold_in(jax.random.fold_in(own_key, 6), axis_at), (blocks,), jnp.float32, smallest / len(pieces), largest / len(pieces))
        return jnp.repeat(jnp.exp(steps), shape[axis_at] // blocks).reshape((-1,) + (1,) * (len(shape) - axis_at - 1))

    factor_of = one(*pieces[0])
    for cut in pieces[1:]:
        factor_of = factor_of * one(*cut)
    return factor_of


def shared_out(stream_key, own, number, rows, number_of, top, reach, skew):
    ranking = jax.random.permutation(stream_key, number_of)
    crowded, usual = load_shares(number_of, rows * top, reach, skew, True), load_shares(number_of, rows * top, reach, skew, False)
    places = jnp.arange(number_of)

    def named(sizes, rotation):
        used = int((sizes > 0).sum())
        fixed = max(1, used // 4)
        shifted = fixed + (places - fixed + rotation * (used - fixed)) % max(1, number_of - fixed)
        return jnp.zeros((number_of,), jnp.int32).at[ranking[jnp.where(places < fixed, places, shifted)]].set(jnp.asarray(sizes, jnp.int32))

    sizes = jnp.where(number % 4 == 0, named(crowded, number // 4), named(usual, number - number // 4 - 1))
    mixed = jax.random.permutation(jax.random.fold_in(own, 3), number_of)
    giver, receiver = mixed[0:number_of // 2 * 2:2], mixed[1:number_of // 2 * 2:2]
    margin = jnp.minimum(sizes[giver] - 1, reach - sizes[receiver]) // 2
    margin = jnp.where((giver == ranking[0]) | (receiver == ranking[0]) | (sizes[receiver] == 0), 0, jnp.maximum(margin, 0))
    shifted = jax.random.randint(jax.random.fold_in(own, 4), (number_of // 2,), 0, 1 << 20) % (margin + 1)
    sizes = sizes.at[giver].add(-shifted).at[receiver].add(shifted)
    labels = jnp.searchsorted(jnp.cumsum(sizes), jnp.arange(rows * top), side="right").astype(jnp.int32)
    grid = labels.reshape(top, rows).T
    grid = grid[jax.random.permutation(jax.random.fold_in(own, 1), rows)]
    rotation = jax.random.randint(jax.random.fold_in(own, 2), (rows, 1), 0, top)
    return jnp.take_along_axis(grid, (jnp.arange(top)[None, :] + rotation) % top, axis=1)


def load_shares(number_of, total, most, lean, full):
    loads = [(1 << 20) // math.isqrt(rank ** lean) + 1 for rank in range(1, number_of + 1)]
    largest = most if full else min(most, max(-(-total // number_of), total * loads[0] // sum(loads)))
    least = 1 if total - largest >= number_of - 1 else 0
    given, spare = [largest] + [least] * (number_of - 1), total - largest - least * (number_of - 1)
    while spare > 0:
        movable = [i for i in range(1, number_of) if given[i] < largest] or [i for i in range(1, number_of) if given[i] < most]
        mass, budget = sum([loads[i] for i in movable]), spare
        for i in movable:
            more = min(most - given[i], max(1, budget * loads[i] // mass), spare)
            given[i] = given[i] + more
            spare = spare - more
    return np.array(given)


def noise(rng, extent, scale, bound, pieces=(), dtype=jnp.bfloat16):
    drawn = scale * jax.random.normal(rng, extent, jnp.float32)
    if pieces:
        drawn = drawn * levels(rng, extent, pieces, -0.22, 0.18)
    return jnp.clip(drawn, -bound, bound).astype(dtype)


def setup_inputs(seed: int = 0) -> dict:
    seeds = jax.random.split(jax.random.key(seed), 9)
    multipoles = noise(seeds[0], (BOXES, RHS, COEFS), 1.0, 6.0, ((0, 128),))
    translations = noise(seeds[1], (TYPES, COEFS, COEFS), (TYPES * COEFS) ** -0.5, 0.0546875)
    local_source = plant(jax.random.randint(seeds[2], (LOCAL_TYPES, BOXES), 0, BOX_DEV), jax.random.fold_in(seeds[2], 1), 0, BOX_DEV - 1).astype(jnp.int32)
    remote_owner_keys = jax.random.split(jax.random.fold_in(seeds[3], 1), (BOXES * REMOTE_TYPES) // REM_TASKS)
    remote_owner_turns = jax.random.permutation(jax.random.fold_in(seeds[3], 3), (BOXES * REMOTE_TYPES) // REM_TASKS)
    remote_owner = jax.vmap(lambda own, number: shared_out(jax.random.fold_in(seeds[3], 2), own, number, REM_TASKS, DEVICES, 1, CAP, 2))(remote_owner_keys, remote_owner_turns).reshape((BOXES * REMOTE_TYPES, 1))
    remote_box = plant(jax.random.randint(seeds[4], (BOXES * REMOTE_TYPES,), 0, BOX_DEV), jax.random.fold_in(seeds[4], 1), 0, BOX_DEV - 1).astype(jnp.int32)
    charges = noise(seeds[5], (RHS, POINTS), 1.0, 6.0, ((1, 128),))
    positions = jnp.clip(jax.random.uniform(seeds[6], (3, POINTS), jnp.float32, -1.0, 1.0) * levels(seeds[6], (3, POINTS), ((1, 128),), -0.4, 0.0), -1.0, 1.0)
    leaf_count = plant(jax.random.randint(seeds[7], (BOXES,), 1, SLOTS + 1), jax.random.fold_in(seeds[7], 1), 1, SLOTS).astype(jnp.int32)
    return dict(multipoles=multipoles, translations=translations, local_source=local_source, remote_owner=remote_owner, remote_box=remote_box, charges=charges, positions=positions, leaf_count=leaf_count)


length_factor = 1.7320508075688772

def node_weights(coord):
    steps = jnp.arange(ORDER).astype(jnp.float32)
    angles = (2.0 * steps + 1.0) * jnp.pi / (2.0 * ORDER)
    theta = jnp.arccos(coord)
    at_point = jnp.cos(theta[..., None] * steps)
    at_node = jnp.cos(angles[:, None] * steps[None, :])
    total = lax.optimization_barrier(jnp.sum(at_point[..., None, :] * at_node, axis=-1))
    return (2.0 * total - 1.0) / ORDER

def interpolate(positions):
    first = node_weights(positions[0])
    second = node_weights(positions[1])
    third = node_weights(positions[2])
    table = first[:, :, None, None] * second[:, None, :, None] * third[:, None, None, :]
    return table.reshape(positions.shape[1], ORDER * ORDER * ORDER)

def near_field(padded, leaves):
    targets = padded[:3, 1:leaves + 1]
    windows = jnp.stack([padded[:, o:o + leaves] for o in range(3)], axis=1)
    source_pos = jnp.transpose(windows[:3], (0, 2, 1, 3))
    diff = targets[:, :, :, None, None] - source_pos[:, :, None, :, :]
    offset = 2.0 * (jnp.arange(3).astype(jnp.float32) - 1.0)
    first = diff[0] - offset[None, None, :, None]
    dist = jnp.sqrt(first * first + diff[1] * diff[1] + diff[2] * diff[2])
    kernel = (1.0 + length_factor * dist) * jnp.exp(-length_factor * dist)
    return jnp.einsum('lqos,rols->rlq', kernel, windows[3:], precision=lax.Precision.HIGHEST)

def reference(multipoles, translations, local_source, remote_owner, remote_box, charges, positions, leaf_count):
    ops = translations.astype(jnp.float32)

    def one_device(device):
        base = (device * BOX_DEV).astype(jnp.int32)
        local_rows = lax.dynamic_slice_in_dim(local_source, base, BOX_DEV, 1) + base
        owner = lax.dynamic_slice_in_dim(remote_owner[:, 0], (device * REM_TASKS).astype(jnp.int32), REM_TASKS, 0)
        boxrow = lax.dynamic_slice_in_dim(remote_box, (device * REM_TASKS).astype(jnp.int32), REM_TASKS, 0)
        remote_rows = (owner * BOX_DEV + boxrow).reshape(REMOTE_TYPES, BOX_DEV)
        index = jnp.concatenate([local_rows, remote_rows], 0).astype(jnp.int32)
        sources = jnp.take(multipoles, index.reshape(-1), axis=0).reshape(TYPES, BOX_DEV, RHS, COEFS).astype(jnp.float32)
        return jnp.einsum('tbrp,tpq->brq', sources, ops, precision=lax.Precision.HIGHEST)
    expansion = lax.map(one_device, jnp.arange(DEVICES).astype(jnp.int32)).reshape(BOXES, RHS, COEFS)
    present = (jnp.arange(SLOTS).astype(jnp.int32)[None, :] < leaf_count[:, None]).astype(jnp.float32)
    weights = interpolate(positions).reshape(BOXES, SLOTS, COEFS)
    far = jnp.einsum('brp,bqp->rbq', expansion, weights, precision=lax.Precision.HIGHEST)
    masked = charges.astype(jnp.float32).reshape(RHS, BOXES, SLOTS) * present[None]
    packed = jnp.concatenate([positions.reshape(3, BOXES, SLOTS), masked], 0)
    padded = jnp.pad(packed, ((0, 0), (1, 1), (0, 0)))
    near = near_field(padded, BOXES)
    potential = ((near + far) * present[None]).reshape(RHS, POINTS)
    return (expansion, potential)
```

```python
import jax
import jax.numpy as jnp
from jax import lax
from jax.experimental import pallas as pl
from jax.experimental.pallas import tpu as pltpu
from jax.sharding import PartitionSpec as P

ORDER = 8
SLOTS = 64
MESH = pl.DeviceIdType.MESH

PARTS = ((0, 0, 0, 512), (1, 16, 0, 512), (2, 32, 0, 512), (0, 48, 0, 128), (1, 48, 128, 128), (2, 48, 256, 256))
ORDERS = ("xyz", "yzx", "zxy")
ROWS = 16


def place(at, core):
    return (at["x"] * 4 + at["z"], at["y"] * 2 + core)


def index_of(at, core):
    return at["x"] * 32 + at["z"] * 8 + at["y"] * 2 + core


def moved(at, axis, step):
    other = dict(at)
    other[axis] = (at[axis] + step) % 4
    return other


def exchange_kernel(owner_ref, box_ref, mult_ref, f0, f1, f2, f3, f4, f5, *scratch):
    finals = (f0, f1, f2, f3, f4, f5)
    gathered, packed, relay = scratch[0:6], scratch[6:12], scratch[12:18]
    ask_v, ask_s = scratch[18:20]
    ask_send, ask_recv, copy_sem, g_send, g_recv, g_own, s_send, s_recv, f_send, f_recv, f_own = scratch[20:]
    slab, sub = lax.axis_index("slab"), lax.axis_index("sub")
    me = {"x": slab // 4, "y": sub // 2, "z": slab % 4}
    core = sub % 2
    mine = index_of(me, core)

    barrier = pltpu.get_barrier_semaphore()
    partners = [(me, 1 - core)]
    for axis in "xyz":
        for step in (1, 3, 2):
            for other in (core, 1 - core):
                partners.append((moved(me, axis, step), other))
    for at, c in partners:
        pl.semaphore_signal(barrier, 1, device_id=place(at, c), device_id_type=MESH)

    owner, box = owner_ref[...], box_ref[...]
    rows = owner.shape[0]
    down = lax.broadcasted_iota(jnp.int32, (rows, rows), 0)
    along = lax.broadcasted_iota(jnp.int32, (rows, rows), 1)
    across = jnp.sum(jnp.where(down == along, owner, 0), axis=0, keepdims=True)
    before = jnp.where((owner == across) & (along < down), 1, 0)
    rank = jnp.sum(before, axis=1, keepdims=True)
    named = owner == lax.broadcasted_iota(jnp.int32, (rows, 128), 1)
    for r in range(2):
        wanted = jnp.sum(jnp.where(named & (rank == r), box, 0), axis=0, keepdims=True)
        ask_v[mine, r : r + 1, :] = wanted

    pl.semaphore_wait(barrier, len(partners))

    def send(src, dst, ssem, rsem, at, c):
        pltpu.make_async_remote_copy(
            src_ref=src, dst_ref=dst, send_sem=ssem, recv_sem=rsem, device_id=place(at, c), device_id_type=MESH
        ).start()

    def drain(ref, sem):
        pltpu.make_async_copy(ref, ref, sem).wait()

    for step in (0, 1, 3, 2):
        for c in (core, 1 - core):
            if step == 0 and c is core:
                continue
            row = ask_v.at[pl.ds(mine, 1)]
            send(row, row, ask_send.at[0], ask_recv.at[0], moved(me, "y", step), c)

    def spread(parts):
        for k in parts:
            order, r0, c0, cols = PARTS[k]
            axis = ORDERS[order][0]
            src = mult_ref.at[:, pl.ds(r0, ROWS), pl.ds(c0, cols)]
            dst = gathered[k].at[pl.ds(me[axis] * 32, 32)]
            pltpu.make_async_copy(src, dst, g_own.at[k]).start()
            for step in (1, 3, 2):
                send(src, dst, g_send.at[k], g_recv.at[k], moved(me, axis, step), core)

    drain(ask_v.at[pl.ds(0, 7)], ask_recv.at[0])
    for step in (1, 3, 2):
        part = ask_v.at[pl.ds(slab * 8, 8)]
        send(part, part, ask_send.at[1], ask_recv.at[1], moved(me, "z", step), core)
    spread((0, 1, 2))
    drain(ask_v.at[pl.ds(0, 24)], ask_recv.at[1])
    for step in (1, 3, 2):
        part = ask_v.at[pl.ds(me["x"] * 32, 32)]
        send(part, part, ask_send.at[2], ask_recv.at[2], moved(me, "x", step), core)
    spread((3, 4, 5))
    drain(ask_v.at[pl.ds(0, 96)], ask_recv.at[2])
    to_scalars = pltpu.make_async_copy(ask_v, ask_s, copy_sem)
    to_scalars.start()
    to_scalars.wait()

    def pack(k):
        order, r0, c0, cols = PARTS[k]
        g, p, q = ORDERS[order]
        drain(gathered[k].at[pl.ds(0, 96)], g_recv.at[k])
        drain(gathered[k].at[pl.ds(0, 32)], g_own.at[k])
        for step in (1, 3, 2, 0):
            target = moved(me, p, step)

            def one(j, _):
                to = dict(target)
                to[q] = j // 8
                asker = index_of(to, (j // 4) % 2)
                source = dict(me)
                source[g] = j % 4
                served = index_of(source, core)
                for r in range(2):
                    row = ask_s[asker, r, served]
                    packed[k][target[p], 2 * j + r] = gathered[k][(j % 4) * 32 + row]
                return 0

            lax.fori_loop(0, 32, one, 0, unroll=4)
            if step:
                send(packed[k].at[target[p]], relay[k].at[me[p]], s_send.at[k], s_recv.at[k, me[p]], target, core)

    def forward(k, step):
        order = PARTS[k][0]
        g, p, q = ORDERS[order]
        came = moved(me, p, step)
        src = packed[k] if step == 0 else relay[k]
        if step:
            drain(relay[k].at[came[p]], s_recv.at[k, came[p]])
        slot = ((came[p] * 4 + me[q]) * 2 + core) * 8
        for hop in (1, 3, 2, 0):
            for c in (core, 1 - core):
                to = moved(me, q, hop)
                piece = src.at[came[p], pl.ds((to[q] * 2 + c) * 8, 8)]
                dst = finals[k].at[pl.ds(slot, 8)]
                if hop == 0 and c is core:
                    pltpu.make_async_copy(piece, dst, f_own.at[k]).start()
                else:
                    send(piece, dst, f_send.at[k], f_recv.at[k], to, c)

    for k in range(6):
        pack(k)
        forward(k, 0)
    for k in range(6):
        for step in (1, 3, 2):
            forward(k, step)

    for k in range(6):
        drain(finals[k].at[pl.ds(0, 224)], f_recv.at[k])
        drain(finals[k].at[pl.ds(0, 32)], f_own.at[k])
        drain(finals[k].at[pl.ds(0, 224)], f_send.at[k])
        drain(packed[k].at[pl.ds(0, 3)], s_send.at[k])
        drain(gathered[k].at[pl.ds(0, 96)], g_send.at[k])
    drain(ask_v.at[pl.ds(0, 7)], ask_send.at[0])
    drain(ask_v.at[pl.ds(0, 24)], ask_send.at[1])
    drain(ask_v.at[pl.ds(0, 96)], ask_send.at[2])


def exchange(owner, box, multipoles):
    any_space = pl.BlockSpec(memory_space=pl.ANY)
    vmem = pl.BlockSpec(memory_space=pltpu.VMEM)
    dma = pltpu.SemaphoreType.DMA
    return pl.pallas_call(
        exchange_kernel,
        out_shape=[jax.ShapeDtypeStruct((256, ROWS, part[3]), jnp.bfloat16) for part in PARTS],
        in_specs=[vmem, vmem, any_space],
        out_specs=[any_space] * 6,
        scratch_shapes=[pltpu.VMEM((128, ROWS, part[3]), jnp.bfloat16) for part in PARTS]
        + [pltpu.VMEM((4, 64, ROWS, part[3]), jnp.bfloat16) for part in PARTS]
        + [pltpu.VMEM((4, 64, ROWS, part[3]), jnp.bfloat16) for part in PARTS]
        + [
            pltpu.VMEM((128, 2, 128), jnp.int32),
            pltpu.SMEM((128, 2, 128), jnp.int32),
            dma((3,)), dma((3,)), dma, dma((6,)), dma((6,)), dma((6,)), dma((6,)), dma((6, 4)), dma((6,)), dma((6,)), dma((6,)),
        ],
        compiler_params=pltpu.CompilerParams(collective_id=0, has_side_effects=True, vmem_limit_bytes=60 * 2**20),
    )(owner, box, multipoles)


def extended(cells, sides, width):
    for axis, dim in sides:
        count = lax.axis_size(axis)
        ends = count - 1
        head = lax.slice_in_dim(cells, 0, width, axis=dim)
        tail = lax.slice_in_dim(cells, cells.shape[dim] - width, cells.shape[dim], axis=dim)
        cells = jnp.concatenate(
            [
                lax.ppermute(tail, axis, [(i, (i + 1) % count) for i in range(ends)]),
                cells,
                lax.ppermute(head, axis, [((i + 1) % count, i) for i in range(ends)]),
            ],
            axis=dim,
        )
    return cells


length_factor = 1.7320508075688772


def extended(cells, sides, width):
    for axis, dim in sides:
        count = lax.axis_size(axis)
        ends = count - 1
        head = lax.slice_in_dim(cells, 0, width, axis=dim)
        tail = lax.slice_in_dim(cells, cells.shape[dim] - width, cells.shape[dim], axis=dim)
        cells = jnp.concatenate(
            [
                lax.ppermute(tail, axis, [(i, (i + 1) % count) for i in range(ends)]),
                cells,
                lax.ppermute(head, axis, [((i + 1) % count, i) for i in range(ends)]),
            ],
            axis=dim,
        )
    return cells


def node_weights(coord):
    steps = jnp.arange(ORDER).astype(jnp.float32)
    angles = (2.0 * steps + 1.0) * jnp.pi / (2.0 * ORDER)
    theta = jnp.arccos(coord)
    at_point = jnp.cos(theta[..., None] * steps)
    at_node = jnp.cos(angles[:, None] * steps[None, :])
    total = jnp.sum(at_point[..., None, :] * at_node, axis=-1)
    return (2.0 * total - 1.0) / ORDER


def interpolate(positions):
    first = node_weights(positions[0])
    second = node_weights(positions[1])
    third = node_weights(positions[2])
    table = first[:, :, None, None] * second[:, None, :, None] * third[:, None, None, :]
    return table.reshape(positions.shape[1], ORDER * ORDER * ORDER)


def near_field(padded, leaves):
    targets = padded[:3, 1 : leaves + 1]
    windows = jnp.stack([padded[:, o : o + leaves] for o in range(3)], axis=1)
    source_pos = jnp.transpose(windows[:3], (0, 2, 1, 3))
    diff = targets[:, :, :, None, None] - source_pos[:, :, None, :, :]
    offset = 2.0 * (jnp.arange(3).astype(jnp.float32) - 1.0)
    first = diff[0] - offset[None, None, :, None]
    dist = jnp.sqrt(first * first + diff[1] * diff[1] + diff[2] * diff[2])
    kernel = (1.0 + length_factor * dist) * jnp.exp(-length_factor * dist)
    return jnp.einsum("lqos,rols->rlq", kernel, windows[3:], precision=lax.Precision.HIGHEST)


def on_device(
    multipoles, translations, local_source, remote_owner, remote_box, charges, positions, leaf_count
):
    boxes, rhs, coefs = multipoles.shape
    local_types = local_source.shape[0]
    remote_types = remote_box.shape[0] // boxes
    local_blocks = jnp.take(multipoles, local_source.reshape(-1), axis=0, mode="clip").reshape(
        local_types, boxes, rhs, coefs
    )
    arrived = exchange(remote_owner, remote_box[:, None], multipoles)
    owner = remote_owner[:, 0]
    rank = jnp.sum(jnp.tril(owner[:, None] == owner[None, :], -1).astype(jnp.int32), axis=1)
    pieces = []
    for (order, _, _, _), part in zip(PARTS, arrived):
        at = {"x": owner // 32, "z": owner // 8 % 4, "y": owner // 2 % 4}
        g, p, q = (at[axis] for axis in ORDERS[order])
        slot = ((p * 4 + q) * 2 + owner % 2) * 8 + g * 2 + rank
        pieces.append(jnp.take(part, slot, axis=0, mode="clip"))
    last = jnp.concatenate(pieces[3:], 2)
    remote_blocks = jnp.concatenate(pieces[:3] + [last], 1).reshape(remote_types, boxes, rhs, coefs)
    sources = jnp.concatenate([local_blocks, remote_blocks], 0)
    expansion = jnp.einsum(
        "tbrp,tpq->brq", sources, translations, preferred_element_type=jnp.float32
    )
    present = (jnp.arange(SLOTS)[None, :] < leaf_count[:, None]).astype(jnp.float32)
    weights = interpolate(positions).reshape(boxes, SLOTS, coefs)
    far = jnp.einsum("brp,bqp->rbq", expansion, weights, precision=lax.Precision.HIGHEST)
    masked = charges.astype(jnp.float32).reshape(rhs, boxes, SLOTS) * present[None]
    packed = jnp.concatenate([positions.reshape(3, boxes, SLOTS), masked], 0)
    padded = extended(packed, ((("slab", "sub"), 1),), 1)
    near = near_field(padded, boxes)
    potential = ((near + far) * present[None]).reshape(rhs, boxes * SLOTS)
    return (expansion, potential)


def solution(mesh):
    placed = (
        P(("slab", "sub"), None, None),
        P(),
        P(None, ("slab", "sub")),
        P(("slab", "sub"), None),
        P(("slab", "sub")),
        P(None, ("slab", "sub")),
        P(None, ("slab", "sub")),
        P(("slab", "sub")),
    )
    return jax.shard_map(
        on_device,
        mesh=mesh,
        in_specs=placed,
        out_specs=(P(("slab", "sub"), None, None), P(None, ("slab", "sub"))),
        check_vma=False,
    )
```

```python
import math

import jax
import jax.numpy as jnp
from jax import lax
from jax.experimental import pallas as pl
from jax.experimental.pallas import tpu as pltpu
from jax.sharding import PartitionSpec as P

ORDER = 8
SLOTS = 64
length_factor = 1.7320508075688772
MESH = pl.DeviceIdType.MESH

PARTS = ((0, 0, 0, 512), (1, 16, 0, 512), (2, 32, 0, 512), (0, 48, 0, 128), (1, 48, 128, 128), (2, 48, 256, 256))
ORDERS = ("xyz", "yzx", "zxy")
ROWS = 16


def place(at, core):
    return (at["x"] * 4 + at["z"], at["y"] * 2 + core)


def index_of(at, core):
    return at["x"] * 32 + at["z"] * 8 + at["y"] * 2 + core


def moved(at, axis, step):
    other = dict(at)
    other[axis] = (at[axis] + step) % 4
    return other


def dot(a, b):
    return jnp.dot(a, b, preferred_element_type=jnp.float32)


def split(value):
    high = value.astype(jnp.bfloat16)
    return high, (value - high.astype(jnp.float32)).astype(jnp.bfloat16)


def whole_kernel(
    owner_ref, box_ref, local_ref, count_ref, mult_ref, ops_ref, charge_ref, pos_ref, expansion_ref, potential_ref, *scratch
):
    relay, scratch = scratch[0:6], scratch[6:]
    gathered, packed, finals = scratch[0:6], scratch[6:12], scratch[12:18]
    ask_v, ask_s, slot_v, slot_s = scratch[18:22]
    mult, ops, stream, total, lhs, charges, places, shifted, columns, tables, edge_out, edge_in = scratch[22:34]
    (ask_send, ask_recv, copy_sem, g_send, g_recv, g_own, s_send, s_recv, f_send, f_recv, f_own) = scratch[34:45]
    load_sem, stream_sem, edge_send, edge_recv, out_sem = scratch[45:]
    loads = [
        pltpu.make_async_copy(charge_ref, charges, load_sem.at[0]),
        pltpu.make_async_copy(pos_ref, places.at[pl.ds(0, 3)], load_sem.at[1]),
        pltpu.make_async_copy(mult_ref, mult, load_sem.at[2]),
        pltpu.make_async_copy(ops_ref.at[pl.ds(16, 8)], ops, load_sem.at[3]),
    ]
    places[...] = jnp.zeros_like(places)
    for load in loads:
        load.start()
    slab, sub = lax.axis_index("slab"), lax.axis_index("sub")
    me = {"x": slab // 4, "y": sub // 2, "z": slab % 4}
    core = sub % 2
    mine = index_of(me, core)

    barrier = pltpu.get_barrier_semaphore()
    partners = [(me, 1 - core)]
    for axis in "xyz":
        for step in (1, 3, 2):
            for other in (core, 1 - core):
                partners.append((moved(me, axis, step), other))
    for z in (1, 3, 2):
        for x in (1, 3, 2):
            partners.append((moved(moved(me, "z", z), "x", x), core))
    for at, c in partners:
        pl.semaphore_signal(barrier, 1, device_id=place(at, c), device_id_type=MESH)
    after, prior = (mine + 1) % 128, (mine + 127) % 128
    for number in (after, prior):
        pl.semaphore_signal(barrier, 1, device_id=(number // 8, number % 8), device_id_type=MESH)

    owner, box = owner_ref[...], box_ref[...]
    rows = owner.shape[0]
    down = lax.broadcasted_iota(jnp.int32, (rows, rows), 0)
    along = lax.broadcasted_iota(jnp.int32, (rows, rows), 1)
    across = jnp.sum(jnp.where(down == along, owner, 0), axis=0, keepdims=True)
    before = jnp.where((owner == across) & (along < down), 1, 0)
    rank = jnp.sum(before, axis=1, keepdims=True)
    row_rank = jnp.sum(jnp.where((owner == across) & (down < along), 1, 0), axis=0, keepdims=True)
    spots = {"x": across // 32, "z": across // 8 % 4, "y": across // 2 % 4}
    for order in range(3):
        g, p, q = (spots[axis] for axis in ORDERS[order])
        slot_v[order : order + 1, :] = ((p * 4 + q) * 2 + across % 2) * 8 + g * 2 + row_rank
    slot_v[3:8, :] = jnp.zeros((5, rows), jnp.int32)
    to_slots = pltpu.make_async_copy(slot_v, slot_s, copy_sem.at[1])
    to_slots.start()
    named = owner == lax.broadcasted_iota(jnp.int32, (rows, 128), 1)
    for r in range(2):
        wanted = jnp.sum(jnp.where(named & (rank == r), box, 0), axis=0, keepdims=True)
        ask_v[mine, r : r + 1, :] = wanted

    pl.semaphore_wait(barrier, len(partners) + 2)

    def send(src, dst, ssem, rsem, at, c):
        pltpu.make_async_remote_copy(
            src_ref=src, dst_ref=dst, send_sem=ssem, recv_sem=rsem, device_id=place(at, c), device_id_type=MESH
        ).start()

    def drain(ref, sem):
        pltpu.make_async_copy(ref, ref, sem).wait()

    lane = lax.broadcasted_iota(jnp.int32, (1, 128), 1)
    second = lane >= 64

    def tile(i):
        return pl.ds(pl.multiple_of(i * 128, 128), 128)

    def present(i):
        return (lane % 64) < jnp.where(second, count_ref[2 * i + 1], count_ref[2 * i])

    def masked(i):
        return jnp.where(present(i), charges[:, tile(i)].astype(jnp.float32), 0.0)

    def send_edges():
        loads[0].wait()
        loads[1].wait()
        for way, (i, number) in enumerate(((15, after), (0, prior))):
            edge_out[way, 0:64, :] = masked(i)
            edge_out[way, 64:72, :] = places[:, tile(i)]
            pltpu.make_async_remote_copy(
                src_ref=edge_out.at[way],
                dst_ref=edge_in.at[way],
                send_sem=edge_send.at[way],
                recv_sem=edge_recv.at[way],
                device_id=(number // 8, number % 8),
                device_id_type=MESH,
            ).start()

    for step in (0, 1, 3, 2):
        for c in (core, 1 - core):
            if step == 0 and c is core:
                continue
            row = ask_v.at[pl.ds(mine, 1)]
            send(row, row, ask_send.at[0], ask_recv.at[0], moved(me, "y", step), c)

    drain(ask_v.at[pl.ds(0, 7)], ask_recv.at[0])
    send_edges()
    for step in (1, 3, 2):
        part = ask_v.at[pl.ds(slab * 8, 8)]
        send(part, part, ask_send.at[1], ask_recv.at[1], moved(me, "z", step), core)
        send(part, part, ask_send.at[1], ask_recv.at[1], moved(me, "x", step), core)
    for z in (1, 3, 2):
        for x in (1, 3, 2):
            part = ask_v.at[pl.ds(slab * 8 + me["y"] * 2, 2)]
            send(part, part, ask_send.at[1], ask_recv.at[1], moved(moved(me, "z", z), "x", x), core)

    def boxes_of(k, at, first, count):
        return gathered[k].at[pl.ds(at[ORDERS[PARTS[k][0]][0]] * 32 + first, count)]

    for k, (order, r0, c0, cols) in enumerate(PARTS):
        axis = ORDERS[order][0]
        src = mult_ref.at[:, pl.ds(r0, ROWS), pl.ds(c0, cols)]
        dst = boxes_of(k, me, 0, 32)
        send(src, dst, g_send.at[k], g_recv.at[k, 0], moved(me, axis, 1), core)
        send(src, dst, g_send.at[k], g_recv.at[k, 1], moved(me, axis, 3), core)
        pltpu.make_async_copy(src, dst, g_own.at[k]).start()
    drain(ask_v.at[pl.ds(0, 66)], ask_recv.at[1])
    to_scalars = pltpu.make_async_copy(ask_v, ask_s, copy_sem.at[0])
    to_scalars.start()
    for k in range(6):
        axis = ORDERS[PARTS[k][0]][0]
        for way, step in ((0, 3), (1, 1)):
            came = moved(me, axis, step)
            drain(boxes_of(k, came, 0, 32), g_recv.at[k, way])
            half = boxes_of(k, came, 16 * way, 16)
            send(half, half, g_send.at[k], g_recv.at[k, 2], moved(me, axis, 4 - step), core)
    to_scalars.wait()

    def pack(k):
        order, r0, c0, cols = PARTS[k]
        g, p, q = ORDERS[order]
        drain(gathered[k].at[pl.ds(0, 32)], g_recv.at[k, 2])
        drain(gathered[k].at[pl.ds(0, 32)], g_own.at[k])
        for step in (1, 3, 2, 0):
            target = moved(me, p, step)

            def one(j, _):
                to = dict(target)
                to[q] = j // 8
                asker = index_of(to, (j // 4) % 2)
                source = dict(me)
                source[g] = j % 4
                served = index_of(source, core)
                for r in range(2):
                    row = ask_s[asker, r, served]
                    packed[k][target[p], 2 * j + r] = gathered[k][(j % 4) * 32 + row]
                return 0

            lax.fori_loop(0, 32, one, 0, unroll=4)
            if step:
                send(packed[k].at[target[p]], relay[k].at[me[p]], s_send.at[k], s_recv.at[k, me[p]], target, core)

    def forward(k, step):
        order = PARTS[k][0]
        g, p, q = ORDERS[order]
        came = moved(me, p, step)
        src = packed[k] if step == 0 else relay[k]
        if step:
            drain(relay[k].at[came[p]], s_recv.at[k, came[p]])
        slot = ((came[p] * 4 + me[q]) * 2 + core) * 8
        for hop in (1, 3, 2, 0):
            for c in (core, 1 - core):
                to = moved(me, q, hop)
                piece = src.at[came[p], pl.ds((to[q] * 2 + c) * 8, 8)]
                dst = finals[k].at[pl.ds(slot, 8)]
                if hop == 0 and c is core:
                    pltpu.make_async_copy(piece, dst, f_own.at[k]).start()
                else:
                    send(piece, dst, f_send.at[k], f_recv.at[k], to, c)

    def near_sums():
        for way in range(2):
            drain(edge_in.at[way], edge_recv.at[way])
            drain(edge_out.at[way], edge_send.at[way])
        here = (mine > 0, mine < 127)
        for way in range(2):
            edge_in[way, 0:64, :] = jnp.where(here[way], edge_in[way, 0:64, :], 0.0)

        def half(i, before, now):
            joined = jnp.where(second, pltpu.roll(now, 64, 1), pltpu.roll(before, 64, 1))
            shifted[:, tile(i)] = joined[0:64].astype(jnp.bfloat16)
            columns[tile(i), 0:8] = jnp.transpose(joined[64:72])

        def own(i):
            return jnp.concatenate([masked(i), places[:, tile(i)]], 0)

        half(0, edge_in[0], own(0))
        half(16, own(15), edge_in[1])

        def middle(i, _):
            half(i, own(i - 1), own(i))
            return 0

        lax.fori_loop(1, 16, middle, 0)

        def pair(i, _):
            kernel_tiles = []
            for sb in range(4):
                o = jnp.where(second, sb - 2, sb - 1)
                at = columns[pl.ds(pl.multiple_of(i * 128 + sb * 64, 64), 64), 0:8]
                dx = places[0:1, tile(i)] - at[:, 0:1] - 2.0 * o.astype(jnp.float32)
                dy = places[1:2, tile(i)] - at[:, 1:2]
                dz = places[2:3, tile(i)] - at[:, 2:3]
                scaled = length_factor * jnp.sqrt(dx * dx + dy * dy + dz * dz)
                value = (1.0 + scaled) * jnp.exp(-scaled)
                kernel_tiles.append(jnp.where((o >= -1) & (o <= 1), value, 0.0))
            high, low = split(jnp.concatenate(kernel_tiles, 0))
            window = shifted[:, pl.ds(pl.multiple_of(i * 128, 128), 256)]
            potential_ref[:, tile(i)] = dot(window, high) + dot(window, low)
            return 0

        lax.fori_loop(0, 16, pair, 0)

    def weight_tables():
        node = lax.broadcasted_iota(jnp.int32, (8, 128), 0)
        factors = []
        for k in range(ORDER):
            column = jnp.zeros((8, 128), jnp.float32)
            for m in range(ORDER):
                column = jnp.where(node == m, math.cos(k * (2 * m + 1) * math.pi / (2 * ORDER)), column)
            factors.append(column)

        def pair(i, _):
            weights = []
            for axis in range(3):
                u = places[axis : axis + 1, tile(i)]
                old, new = jnp.ones_like(u), u
                value = factors[0] + factors[1] * u
                for k in range(2, ORDER):
                    old, new = new, 2.0 * u * new - old
                    value = value + factors[k] * new
                weights.append((2.0 * value - 1.0) / ORDER)
            for m1 in range(ORDER):
                parts = [(weights[0][m1 : m1 + 1] * weights[1][m2 : m2 + 1]) * weights[2] for m2 in range(ORDER)]
                high, low = split(jnp.concatenate(parts, 0))
                tables[i, m1 * 64 : m1 * 64 + 64, 0:128] = high
                tables[i, m1 * 64 : m1 * 64 + 64, 128:256] = low
            return 0

        lax.fori_loop(0, 16, pair, 0)

    def load_op(t):
        return pltpu.make_async_copy(ops_ref.at[t], stream.at[t % 2], stream_sem.at[t % 2])

    def local_type(t):
        load_op(t).wait()
        if t + 1 < 16:
            load_op(t + 1).start()

        def group(i, _):
            for b in range(8):
                lhs[b * 64 : b * 64 + 64, :] = mult[local_ref[t, i * 8 + b]]
            value = dot(lhs[...], stream[t % 2]).reshape(8, 64, 512)
            if t == 0:
                total[pl.ds(i * 8, 8)] = value
            else:
                total[pl.ds(i * 8, 8)] += value
            return 0

        lax.fori_loop(0, 4, group, 0)

    def remote_rows(parts):
        r0 = PARTS[parts[0]][1]
        for k in parts:
            drain(finals[k].at[pl.ds(0, 224)], f_recv.at[k])
            drain(finals[k].at[pl.ds(0, 32)], f_own.at[k])

        def one(t, _):
            at = 0
            for k in parts:
                order, _, c0, cols = PARTS[k]
                for b in range(32):
                    lhs[b * 16 : b * 16 + 16, c0 : c0 + cols] = finals[k][slot_s[order, t * 32 + b]]
            total[:, r0 : r0 + ROWS, :] += dot(lhs[...], ops[t]).reshape(32, ROWS, 512)
            return 0

        lax.fori_loop(0, 8, one, 0)

    def store_rows(r0, count):
        return pltpu.make_async_copy(
            total.at[:, pl.ds(r0, count)], expansion_ref.at[:, pl.ds(r0, count)], out_sem.at[r0 // 48]
        )

    def far_rows(r0, count):
        def pair(i, _):
            value = total[pl.ds(2 * i, 2), r0 : r0 + count, :].reshape(2 * count, 512)
            high, low = split(value)
            both = dot(jnp.concatenate([high, low], 0), tables[i])
            summed = both[: 2 * count, 0:128] + both[: 2 * count, 128:256] + both[2 * count :, 0:128]
            far = jnp.where(second, summed[count:], summed[:count])
            near = potential_ref[r0 : r0 + count, tile(i)]
            potential_ref[r0 : r0 + count, tile(i)] = jnp.where(present(i), near + far, 0.0)
            return 0

        lax.fori_loop(0, 16, pair, 0)

    load_op(0).start()
    for k in range(6):
        pack(k)
        forward(k, 0)
    near_sums()
    weight_tables()
    loads[2].wait()
    t = 0
    for ks in ((0, 1, 2), (3, 4, 5)):
        for step in (1, 3, 2):
            for k in ks:
                forward(k, step)
                if t < 16:
                    local_type(t)
                    t += 1
    loads[3].wait()
    to_slots.wait()
    for k in range(3):
        remote_rows((k,))
    store_rows(0, 48).start()
    far_rows(0, 48)
    remote_rows((3, 4, 5))
    store_rows(48, 16).start()
    far_rows(48, 16)
    store_rows(0, 48).wait()
    store_rows(48, 16).wait()
    for k in range(6):
        drain(finals[k].at[pl.ds(0, 224)], f_send.at[k])
        drain(packed[k].at[pl.ds(0, 3)], s_send.at[k])
        drain(gathered[k].at[pl.ds(0, 96)], g_send.at[k])
    drain(ask_v.at[pl.ds(0, 7)], ask_send.at[0])
    drain(ask_v.at[pl.ds(0, 66)], ask_send.at[1])


def on_device(
    multipoles, translations, local_source, remote_owner, remote_box, charges, positions, leaf_count
):
    any_space = pl.BlockSpec(memory_space=pl.ANY)
    vmem = pl.BlockSpec(memory_space=pltpu.VMEM)
    smem = pl.BlockSpec(memory_space=pltpu.SMEM)
    dma = pltpu.SemaphoreType.DMA
    bf16, f32, i32 = jnp.bfloat16, jnp.float32, jnp.int32
    results = pl.pallas_call(
        whole_kernel,
        out_shape=[
            jax.ShapeDtypeStruct((32, 64, 512), f32),
            jax.ShapeDtypeStruct((64, 2048), f32),
        ]
        + [jax.ShapeDtypeStruct((4, 64, ROWS, part[3]), bf16) for part in PARTS],
        in_specs=[vmem, vmem, smem, smem, any_space, any_space, any_space, any_space],
        out_specs=[any_space, vmem] + [any_space] * 6,
        scratch_shapes=[pltpu.VMEM((128, ROWS, part[3]), bf16) for part in PARTS]
        + [pltpu.VMEM((4, 64, ROWS, part[3]), bf16) for part in PARTS]
        + [pltpu.VMEM((256, ROWS, part[3]), bf16) for part in PARTS]
        + [
            pltpu.VMEM((128, 2, 128), i32),
            pltpu.SMEM((128, 2, 128), i32),
            pltpu.VMEM((8, 256), i32),
            pltpu.SMEM((8, 256), i32),
            pltpu.VMEM((32, 64, 512), bf16),
            pltpu.VMEM((8, 512, 512), bf16),
            pltpu.VMEM((2, 512, 512), bf16),
            pltpu.VMEM((32, 64, 512), f32),
            pltpu.VMEM((512, 512), bf16),
            pltpu.VMEM((64, 2048), bf16),
            pltpu.VMEM((8, 2048), f32),
            pltpu.VMEM((64, 2176), bf16),
            pltpu.VMEM((2176, 8), f32),
            pltpu.VMEM((16, 512, 256), bf16),
            pltpu.VMEM((2, 72, 128), f32),
            pltpu.VMEM((2, 72, 128), f32),
            dma((2,)), dma((2,)), dma((2,)), dma((6,)), dma((6, 3)), dma((6,)), dma((6,)), dma((6, 4)), dma((6,)), dma((6,)), dma((6,)),
            dma((4,)), dma((2,)), dma((2,)), dma((2,)), dma((2,)),
        ],
        compiler_params=pltpu.CompilerParams(collective_id=0, has_side_effects=True, vmem_limit_bytes=62 * 2**20),
    )(remote_owner, remote_box[:, None], local_source, leaf_count, multipoles, translations, charges, positions)
    return results[0], results[1]


def solution(mesh):
    placed = (
        P(("slab", "sub"), None, None),
        P(),
        P(None, ("slab", "sub")),
        P(("slab", "sub"), None),
        P(("slab", "sub")),
        P(None, ("slab", "sub")),
        P(None, ("slab", "sub")),
        P(("slab", "sub")),
    )
    return jax.shard_map(
        on_device,
        mesh=mesh,
        in_specs=placed,
        out_specs=(P(("slab", "sub"), None, None), P(None, ("slab", "sub"))),
        check_vma=False,
    )
```

```python
import math

import jax
import jax.numpy as jnp
from jax import lax
from jax.experimental import pallas as pl
from jax.experimental.pallas import tpu as pltpu
from jax.sharding import PartitionSpec as P

ORDER = 8
SLOTS = 64
length_factor = 1.7320508075688772
MESH = pl.DeviceIdType.MESH

PARTS = ((0, 0, 0, 512), (1, 16, 0, 512), (2, 32, 0, 512), (0, 48, 0, 128), (1, 48, 128, 128), (2, 48, 256, 256))
ORDERS = ("xyz", "yzx", "zxy")
ROWS = 16


def place(at, core):
    return (at["x"] * 4 + at["z"], at["y"] * 2 + core)


def index_of(at, core):
    return at["x"] * 32 + at["z"] * 8 + at["y"] * 2 + core


def moved(at, axis, step):
    other = dict(at)
    other[axis] = (at[axis] + step) % 4
    return other


def dot(a, b):
    return jnp.dot(a, b, preferred_element_type=jnp.float32)


def split(value):
    high = value.astype(jnp.bfloat16)
    return high, (value - high.astype(jnp.float32)).astype(jnp.bfloat16)


def whole_kernel(
    owner_ref, box_ref, local_hbm, count_hbm, mult_ref, ops_ref, charge_ref, pos_ref, expansion_ref, potential_ref, *scratch
):
    relay, scratch = scratch[0:6], scratch[6:]
    gathered, packed, finals = scratch[0:6], scratch[6:12], scratch[12:18]
    ask_v, ask_s, slot_v, slot_s = scratch[18:22]
    mult, ops, stream, total, lhs, charges, places, shifted, columns, tables, edge_out, edge_in = scratch[22:34]
    asked, local_ref, count_ref = scratch[34:37]
    scratch = scratch[0:34] + scratch[37:]
    (ask_send, ask_recv, copy_sem, g_send, g_recv, g_own, s_send, s_recv, f_send, f_recv, f_own) = scratch[34:45]
    load_sem, stream_sem, edge_send, edge_recv, out_sem = scratch[45:]
    loads = [
        pltpu.make_async_copy(local_hbm, local_ref, load_sem.at[4]),
        pltpu.make_async_copy(count_hbm, count_ref, load_sem.at[5]),
        pltpu.make_async_copy(owner_ref, asked.at[0], load_sem.at[6]),
        pltpu.make_async_copy(box_ref, asked.at[1], load_sem.at[7]),
        pltpu.make_async_copy(charge_ref, charges, load_sem.at[0]),
        pltpu.make_async_copy(pos_ref, places.at[pl.ds(0, 3)], load_sem.at[1]),
        pltpu.make_async_copy(mult_ref, mult, load_sem.at[2]),
        pltpu.make_async_copy(ops_ref.at[pl.ds(4, 2)], ops, load_sem.at[3]),
    ]
    places[...] = jnp.zeros_like(places)
    for load in loads:
        load.start()
    slab, sub = lax.axis_index("slab"), lax.axis_index("sub")
    me = {"x": slab // 4, "y": sub // 2, "z": slab % 4}
    core = sub % 2
    mine = index_of(me, core)

    barrier = pltpu.get_barrier_semaphore()
    partners = [(me, 1 - core)]
    for axis in "xyz":
        for step in (1, 3, 2):
            for other in (core, 1 - core):
                partners.append((moved(me, axis, step), other))
    for z in (1, 3, 2):
        for x in (1, 3, 2):
            partners.append((moved(moved(me, "z", z), "x", x), core))
    for at, c in partners:
        pl.semaphore_signal(barrier, 1, device_id=place(at, c), device_id_type=MESH)
    after, prior = (mine + 1) % 128, (mine + 127) % 128
    for number in (after, prior):
        pl.semaphore_signal(barrier, 1, device_id=(number // 8, number % 8), device_id_type=MESH)

    loads[2].wait()
    loads[3].wait()
    rows = 256
    down = lax.broadcasted_iota(jnp.int32, (rows, rows), 0)
    along = lax.broadcasted_iota(jnp.int32, (rows, rows), 1)
    across = jnp.concatenate([asked[0, 0:1, :], asked[0, 1:2, :]], 1)
    boxes_across = jnp.concatenate([asked[1, 0:1, :], asked[1, 1:2, :]], 1)
    owner = jnp.sum(jnp.where(down == along, across, 0), axis=1, keepdims=True)
    box = jnp.sum(jnp.where(down == along, boxes_across, 0), axis=1, keepdims=True)
    before = jnp.where((owner == across) & (along < down), 1, 0)
    rank = jnp.sum(before, axis=1, keepdims=True)
    row_rank = jnp.sum(jnp.where((owner == across) & (down < along), 1, 0), axis=0, keepdims=True)
    spots = {"x": across // 32, "z": across // 8 % 4, "y": across // 2 % 4}
    for order in range(3):
        g, p, q = (spots[axis] for axis in ORDERS[order])
        slot_v[order : order + 1, :] = ((p * 4 + q) * 2 + across % 2) * 8 + g * 2 + row_rank
    slot_v[3:8, :] = jnp.zeros((5, rows), jnp.int32)
    to_slots = pltpu.make_async_copy(slot_v, slot_s, copy_sem.at[1])
    to_slots.start()
    named = owner == lax.broadcasted_iota(jnp.int32, (rows, 128), 1)
    for r in range(2):
        wanted = jnp.sum(jnp.where(named & (rank == r), box, 0), axis=0, keepdims=True)
        ask_v[mine, r : r + 1, :] = wanted

    pl.semaphore_wait(barrier, len(partners) + 2)

    def send(src, dst, ssem, rsem, at, c):
        pltpu.make_async_remote_copy(
            src_ref=src, dst_ref=dst, send_sem=ssem, recv_sem=rsem, device_id=place(at, c), device_id_type=MESH
        ).start()

    def drain(ref, sem):
        pltpu.make_async_copy(ref, ref, sem).wait()

    lane = lax.broadcasted_iota(jnp.int32, (1, 128), 1)
    second = lane >= 64

    def tile(i):
        return pl.ds(pl.multiple_of(i * 128, 128), 128)

    def present(i):
        return (lane % 64) < jnp.where(second, count_ref[2 * i + 1], count_ref[2 * i])

    def masked(i):
        return jnp.where(present(i), charges[:, tile(i)].astype(jnp.float32), 0.0)

    def send_edges():
        loads[1].wait()
        loads[4].wait()
        loads[5].wait()
        for way, (i, number) in enumerate(((15, after), (0, prior))):
            edge_out[way, 0:64, :] = masked(i)
            edge_out[way, 64:72, :] = places[:, tile(i)]
            pltpu.make_async_remote_copy(
                src_ref=edge_out.at[way],
                dst_ref=edge_in.at[way],
                send_sem=edge_send.at[way],
                recv_sem=edge_recv.at[way],
                device_id=(number // 8, number % 8),
                device_id_type=MESH,
            ).start()

    for step in (0, 1, 3, 2):
        for c in (core, 1 - core):
            if step == 0 and c is core:
                continue
            row = ask_v.at[pl.ds(mine, 1)]
            send(row, row, ask_send.at[0], ask_recv.at[0], moved(me, "y", step), c)

    def boxes_of(k, at, first, count):
        return gathered[k].at[pl.ds(at[ORDERS[PARTS[k][0]][0]] * 32 + first, count)]

    def spread(k, first, count, step, sem):
        order, r0, c0, cols = PARTS[k]
        src = mult_ref.at[pl.ds(first, count), pl.ds(r0, ROWS), pl.ds(c0, cols)]
        dst = boxes_of(k, me, first, count)
        send(src, dst, g_send.at[k], g_recv.at[k, sem], moved(me, ORDERS[order][0], step), core)

    def pass_on(k):
        axis = ORDERS[PARTS[k][0]][0]
        for way, step in ((0, 3), (1, 1)):
            came = moved(me, axis, step)
            half = boxes_of(k, came, 16 * way, 16)
            drain(half, g_recv.at[k, way])
            send(half, half, g_send.at[k], g_recv.at[k, 2], moved(me, axis, 4 - step), core)

    for k in range(3):
        spread(k, 0, 16, 1, 0)
        spread(k, 16, 16, 3, 1)
    send_edges()
    drain(ask_v.at[pl.ds(0, 7)], ask_recv.at[0])
    for step in (1, 3, 2):
        part = ask_v.at[pl.ds(slab * 8, 8)]
        send(part, part, ask_send.at[1], ask_recv.at[1], moved(me, "z", step), core)
        send(part, part, ask_send.at[1], ask_recv.at[1], moved(me, "x", step), core)
    for z in (1, 3, 2):
        for x in (1, 3, 2):
            part = ask_v.at[pl.ds(slab * 8 + me["y"] * 2, 2)]
            send(part, part, ask_send.at[1], ask_recv.at[1], moved(moved(me, "z", z), "x", x), core)
    for k in range(3):
        spread(k, 16, 16, 1, 2)
        spread(k, 0, 16, 3, 2)
    for k, (order, r0, c0, cols) in enumerate(PARTS):
        own_boxes = mult_ref.at[:, pl.ds(r0, ROWS), pl.ds(c0, cols)]
        pltpu.make_async_copy(own_boxes, boxes_of(k, me, 0, 32), g_own.at[k]).start()
    for k in range(3):
        pass_on(k)
    for k in range(3, 6):
        spread(k, 0, 16, 1, 0)
        spread(k, 16, 16, 3, 1)
        spread(k, 16, 16, 1, 2)
        spread(k, 0, 16, 3, 2)
    drain(ask_v.at[pl.ds(0, 66)], ask_recv.at[1])
    to_scalars = pltpu.make_async_copy(ask_v, ask_s, copy_sem.at[0])
    to_scalars.start()
    to_scalars.wait()

    def pack(k, steps):
        order, r0, c0, cols = PARTS[k]
        g, p, q = ORDERS[order]
        for step in steps:
            target = moved(me, p, step)

            def one(j, _):
                to = dict(target)
                to[q] = j // 8
                asker = index_of(to, (j // 4) % 2)
                source = dict(me)
                source[g] = j % 4
                served = index_of(source, core)
                for r in range(2):
                    row = ask_s[asker, r, served]
                    packed[k][target[p], 2 * j + r] = gathered[k][(j % 4) * 32 + row]
                return 0

            lax.fori_loop(0, 32, one, 0, unroll=4)
            if step:
                send(packed[k].at[target[p]], relay[k].at[me[p]], s_send.at[k], s_recv.at[k, me[p]], target, core)

    def boxes_are_here(k):
        drain(gathered[k].at[pl.ds(0, 64)], g_recv.at[k, 2])
        drain(gathered[k].at[pl.ds(0, 32)], g_own.at[k])

    def forward(k, step):
        order = PARTS[k][0]
        g, p, q = ORDERS[order]
        came = moved(me, p, step)
        src = packed[k] if step == 0 else relay[k]
        if step:
            drain(relay[k].at[came[p]], s_recv.at[k, came[p]])
        slot = ((came[p] * 4 + me[q]) * 2 + core) * 8
        for hop in (1, 3, 2, 0):
            for c in (core, 1 - core):
                to = moved(me, q, hop)
                piece = src.at[came[p], pl.ds((to[q] * 2 + c) * 8, 8)]
                dst = finals[k].at[pl.ds(slot, 8)]
                if hop == 0 and c is core:
                    pltpu.make_async_copy(piece, dst, f_own.at[k]).start()
                else:
                    send(piece, dst, f_send.at[k], f_recv.at[k], to, c)

    def near_sums():
        for way in range(2):
            drain(edge_in.at[way], edge_recv.at[way])
            drain(edge_out.at[way], edge_send.at[way])
        here = (mine > 0, mine < 127)
        for way in range(2):
            edge_in[way, 0:64, :] = jnp.where(here[way], edge_in[way, 0:64, :], 0.0)

        def half(i, before, now):
            joined = jnp.where(second, pltpu.roll(now, 64, 1), pltpu.roll(before, 64, 1))
            shifted[:, tile(i)] = joined[0:64].astype(jnp.bfloat16)
            columns[tile(i), 0:8] = jnp.transpose(joined[64:72])

        def own(i):
            return jnp.concatenate([masked(i), places[:, tile(i)]], 0)

        half(0, edge_in[0], own(0))
        half(16, own(15), edge_in[1])

        def middle(i, _):
            half(i, own(i - 1), own(i))
            return 0

        lax.fori_loop(1, 16, middle, 0)

        def pair(i, _):
            kernel_tiles = []
            for sb in range(4):
                o = jnp.where(second, sb - 2, sb - 1)
                at = columns[pl.ds(pl.multiple_of(i * 128 + sb * 64, 64), 64), 0:8]
                dx = places[0:1, tile(i)] - at[:, 0:1] - 2.0 * o.astype(jnp.float32)
                dy = places[1:2, tile(i)] - at[:, 1:2]
                dz = places[2:3, tile(i)] - at[:, 2:3]
                scaled = length_factor * jnp.sqrt(dx * dx + dy * dy + dz * dz)
                value = (1.0 + scaled) * jnp.exp(-scaled)
                kernel_tiles.append(jnp.where((o >= -1) & (o <= 1), value, 0.0))
            high, low = split(jnp.concatenate(kernel_tiles, 0))
            window = shifted[:, pl.ds(pl.multiple_of(i * 128, 128), 256)]
            potential_ref[:, tile(i)] = dot(window, high) + dot(window, low)
            return 0

        lax.fori_loop(0, 16, pair, 0)

    def weight_tables():
        node = lax.broadcasted_iota(jnp.int32, (8, 128), 0)
        factors = []
        for k in range(ORDER):
            column = jnp.zeros((8, 128), jnp.float32)
            for m in range(ORDER):
                column = jnp.where(node == m, math.cos(k * (2 * m + 1) * math.pi / (2 * ORDER)), column)
            factors.append(column)

        def pair(i, _):
            weights = []
            for axis in range(3):
                u = places[axis : axis + 1, tile(i)]
                old, new = jnp.ones_like(u), u
                value = factors[0] + factors[1] * u
                for k in range(2, ORDER):
                    old, new = new, 2.0 * u * new - old
                    value = value + factors[k] * new
                weights.append((2.0 * value - 1.0) / ORDER)
            for m1 in range(ORDER):
                parts = [(weights[0][m1 : m1 + 1] * weights[1][m2 : m2 + 1]) * weights[2] for m2 in range(ORDER)]
                high, low = split(jnp.concatenate(parts, 0))
                tables[i, m1 * 64 : m1 * 64 + 64, 0:128] = high
                tables[i, m1 * 64 : m1 * 64 + 64, 128:256] = low
            return 0

        lax.fori_loop(0, 16, pair, 0)

    def load_op(t):
        return pltpu.make_async_copy(
            ops_ref.at[t // 4, pl.ds(t % 4 * 512, 512)], stream.at[t % 2], stream_sem.at[t % 2]
        )

    def local_type(t):
        load_op(t).wait()
        if t + 1 < 16:
            load_op(t + 1).start()

        def group(i, _):
            for b in range(8):
                lhs[b * 64 : b * 64 + 64, 0:512] = mult[local_ref[t, i * 8 + b]]
            value = dot(lhs[:, 0:512], stream[t % 2]).reshape(8, 64, 512)
            if t == 0:
                total[pl.ds(i * 8, 8)] = value
            else:
                total[pl.ds(i * 8, 8)] += value
            return 0

        lax.fori_loop(0, 4, group, 0)

    def remote_rows(parts):
        r0 = PARTS[parts[0]][1]
        for k in parts:
            drain(finals[k].at[pl.ds(0, 224)], f_recv.at[k])
            drain(finals[k].at[pl.ds(0, 32)], f_own.at[k])

        def one(t, _):
            for k in parts:
                order, _, c0, cols = PARTS[k]
                for half in range(4):
                    for b in range(32):
                        at = pl.ds(half * 512 + c0, cols)
                        lhs[b * 16 : b * 16 + 16, at] = finals[k][slot_s[order, (4 * t + half) * 32 + b]]
            total[:, r0 : r0 + ROWS, :] += dot(lhs[...], ops[t]).reshape(32, ROWS, 512)
            return 0

        lax.fori_loop(0, 2, one, 0)

    def store_rows(r0, count):
        return pltpu.make_async_copy(
            total.at[:, pl.ds(r0, count)], expansion_ref.at[:, pl.ds(r0, count)], out_sem.at[r0 // 48]
        )

    def far_rows(r0, count):
        def pair(i, _):
            value = total[pl.ds(2 * i, 2), r0 : r0 + count, :].reshape(2 * count, 512)
            high, low = split(value)
            both = dot(jnp.concatenate([high, low], 0), tables[i])
            summed = (both[: 2 * count, 0:128] + both[: 2 * count, 128:256]) + (both[2 * count :, 0:128] + both[2 * count :, 128:256])
            far = jnp.where(second, summed[count:], summed[:count])
            near = potential_ref[r0 : r0 + count, tile(i)]
            potential_ref[r0 : r0 + count, tile(i)] = jnp.where(present(i), near + far, 0.0)
            return 0

        lax.fori_loop(0, 16, pair, 0)

    load_op(0).start()
    for k in range(3):
        boxes_are_here(k)
        pack(k, (1, 3))
    for k in range(3, 6):
        pass_on(k)
    for k in range(3):
        pack(k, (2, 0))
    near_sums()
    weight_tables()
    loads[0].wait()
    loads[6].wait()
    for t in range(4):
        local_type(t)
    for k in range(3, 6):
        boxes_are_here(k)
        pack(k, (1, 3, 2, 0))
    t = 4
    for ks in ((0, 1, 2), (3, 4, 5)):
        for step in (0, 1, 3, 2):
            for k in ks:
                forward(k, step)
            if t < 16:
                local_type(t)
                local_type(t + 1)
                t += 2
    loads[7].wait()
    to_slots.wait()
    for k in range(3):
        remote_rows((k,))
    store_rows(0, 48).start()
    far_rows(0, 48)
    remote_rows((3, 4, 5))
    store_rows(48, 16).start()
    far_rows(48, 16)
    store_rows(0, 48).wait()
    store_rows(48, 16).wait()
    for k in range(6):
        drain(finals[k].at[pl.ds(0, 224)], f_send.at[k])
        drain(packed[k].at[pl.ds(0, 3)], s_send.at[k])
        drain(gathered[k].at[pl.ds(0, 96)], g_send.at[k])
    drain(ask_v.at[pl.ds(0, 7)], ask_send.at[0])
    drain(ask_v.at[pl.ds(0, 66)], ask_send.at[1])


def on_device(
    multipoles, translations, local_source, remote_owner, remote_box, charges, positions, leaf_count
):
    any_space = pl.BlockSpec(memory_space=pl.ANY)
    vmem = pl.BlockSpec(memory_space=pltpu.VMEM)
    dma = pltpu.SemaphoreType.DMA
    bf16, f32, i32 = jnp.bfloat16, jnp.float32, jnp.int32
    results = pl.pallas_call(
        whole_kernel,
        out_shape=[
            jax.ShapeDtypeStruct((32, 64, 512), f32),
            jax.ShapeDtypeStruct((64, 2048), f32),
        ]
        + [jax.ShapeDtypeStruct((4, 64, ROWS, part[3]), bf16) for part in PARTS],
        in_specs=[any_space] * 8,
        out_specs=[any_space, vmem] + [any_space] * 6,
        scratch_shapes=[pltpu.VMEM((128, ROWS, part[3]), bf16) for part in PARTS]
        + [pltpu.VMEM((4, 64, ROWS, part[3]), bf16) for part in PARTS]
        + [pltpu.VMEM((256, ROWS, part[3]), bf16) for part in PARTS]
        + [
            pltpu.VMEM((128, 2, 128), i32),
            pltpu.SMEM((128, 2, 128), i32),
            pltpu.VMEM((8, 256), i32),
            pltpu.SMEM((8, 256), i32),
            pltpu.VMEM((32, 64, 512), bf16),
            pltpu.VMEM((2, 2048, 512), bf16),
            pltpu.VMEM((2, 512, 512), bf16),
            pltpu.VMEM((32, 64, 512), f32),
            pltpu.VMEM((512, 2048), bf16),
            pltpu.VMEM((64, 2048), bf16),
            pltpu.VMEM((8, 2048), f32),
            pltpu.VMEM((64, 2176), bf16),
            pltpu.VMEM((2176, 8), f32),
            pltpu.VMEM((16, 512, 256), bf16),
            pltpu.VMEM((2, 72, 128), f32),
            pltpu.VMEM((2, 72, 128), f32),
            pltpu.VMEM((2, 2, 128), i32),
            pltpu.SMEM((16, 32), i32),
            pltpu.SMEM((32,), i32),
            dma((2,)), dma((2,)), dma((2,)), dma((6,)), dma((6, 3)), dma((6,)), dma((6,)), dma((6, 4)), dma((6,)), dma((6,)), dma((6,)),
            dma((8,)), dma((2,)), dma((2,)), dma((2,)), dma((2,)),
        ],
        compiler_params=pltpu.CompilerParams(collective_id=0, has_side_effects=True, vmem_limit_bytes=62 * 2**20),
    )(remote_owner.reshape(2, 128), remote_box.reshape(2, 128), local_source, leaf_count, multipoles, translations.reshape(6, 2048, 512), charges, positions)
    return results[0], results[1]


def solution(mesh):
    placed = (
        P(("slab", "sub"), None, None),
        P(),
        P(None, ("slab", "sub")),
        P(("slab", "sub"), None),
        P(("slab", "sub")),
        P(None, ("slab", "sub")),
        P(None, ("slab", "sub")),
        P(("slab", "sub")),
    )
    return jax.shard_map(
        on_device,
        mesh=mesh,
        in_specs=placed,
        out_specs=(P(("slab", "sub"), None, None), P(None, ("slab", "sub"))),
        check_vma=False,
    )
```

```python
import math

import jax
import jax.numpy as jnp
from jax import lax
from jax.experimental import pallas as pl
from jax.experimental.pallas import tpu as pltpu
from jax.sharding import PartitionSpec as P

ORDER = 8
SLOTS = 64
length_factor = 1.7320508075688772
MESH = pl.DeviceIdType.MESH

PARTS = ((0, 0, 0, 512), (1, 16, 0, 512), (2, 32, 0, 512), (0, 48, 0, 128), (1, 48, 128, 128), (2, 48, 256, 256))
ORDERS = ("xyz", "yzx", "zxy")
ROWS = 16


def place(at, core):
    return (at["x"] * 4 + at["z"], at["y"] * 2 + core)


def index_of(at, core):
    return at["x"] * 32 + at["z"] * 8 + at["y"] * 2 + core


def moved(at, axis, step):
    other = dict(at)
    other[axis] = (at[axis] + step) % 4
    return other


def dot(a, b):
    return jnp.dot(a, b, preferred_element_type=jnp.float32)


def split(value):
    high = value.astype(jnp.bfloat16)
    return high, (value - high.astype(jnp.float32)).astype(jnp.bfloat16)


def whole_kernel(
    owner_ref, box_ref, local_hbm, count_hbm, mult_ref, ops_ref, charge_ref, pos_ref, expansion_ref, potential_ref, *scratch
):
    relay, scratch = scratch[0:6], scratch[6:]
    gathered, packed, finals = scratch[0:6], scratch[6:12], scratch[12:18]
    ask_v, ask_s, slot_v, slot_s = scratch[18:22]
    mult, ops, stream, lhs, charges, places, shifted, columns, tables, edge_out, edge_in = scratch[22:33]
    asked, local_ref, count_ref = scratch[33:36]
    total = expansion_ref
    scratch = scratch[0:33] + scratch[36:]
    (ask_send, ask_recv, copy_sem, g_send, g_recv, g_own, s_send, s_recv, f_send, f_recv, f_own) = scratch[33:44]
    load_sem, stream_sem, edge_send, edge_recv = scratch[44:]
    slab, sub = lax.axis_index("slab"), lax.axis_index("sub")
    me = {"x": slab // 4, "y": sub // 2, "z": slab % 4}
    core = sub % 2
    mine = index_of(me, core)

    barrier = pltpu.get_barrier_semaphore()
    partners = [(me, 1 - core)]
    for axis in "xyz":
        for step in (1, 3, 2):
            for other in (core, 1 - core):
                partners.append((moved(me, axis, step), other))
    for z in (1, 3, 2):
        for x in (1, 3, 2):
            partners.append((moved(moved(me, "z", z), "x", x), core))
    for at, c in partners:
        pl.semaphore_signal(barrier, 1, device_id=place(at, c), device_id_type=MESH)
    after, prior = (mine + 1) % 128, (mine + 127) % 128
    for number in (after, prior):
        pl.semaphore_signal(barrier, 1, device_id=(number // 8, number % 8), device_id_type=MESH)

    loads = [
        pltpu.make_async_copy(local_hbm, local_ref, load_sem.at[4]),
        pltpu.make_async_copy(count_hbm, count_ref, load_sem.at[5]),
        pltpu.make_async_copy(owner_ref, asked.at[0], load_sem.at[6]),
        pltpu.make_async_copy(box_ref, asked.at[1], load_sem.at[7]),
        pltpu.make_async_copy(charge_ref, charges, load_sem.at[0]),
        pltpu.make_async_copy(pos_ref, places.at[pl.ds(0, 3)], load_sem.at[1]),
        pltpu.make_async_copy(mult_ref, mult, load_sem.at[2]),
        pltpu.make_async_copy(ops_ref.at[pl.ds(4, 2)], ops, load_sem.at[3]),
    ]
    places[...] = jnp.zeros_like(places)
    for load in loads:
        load.start()
    pl.semaphore_wait(barrier, len(partners) + 2)

    def send(src, dst, ssem, rsem, at, c):
        pltpu.make_async_remote_copy(
            src_ref=src, dst_ref=dst, send_sem=ssem, recv_sem=rsem, device_id=place(at, c), device_id_type=MESH
        ).start()

    def drain(ref, sem):
        pltpu.make_async_copy(ref, ref, sem).wait()

    lane = lax.broadcasted_iota(jnp.int32, (1, 128), 1)
    second = lane >= 64

    def tile(i):
        return pl.ds(pl.multiple_of(i * 128, 128), 128)

    def present(i):
        return (lane % 64) < jnp.where(second, count_ref[2 * i + 1], count_ref[2 * i])

    def masked(i):
        return jnp.where(present(i), charges[:, tile(i)].astype(jnp.float32), 0.0)

    def send_edges():
        loads[1].wait()
        loads[4].wait()
        loads[5].wait()
        for way, (i, number) in enumerate(((15, after), (0, prior))):
            edge_out[way, 0:64, :] = masked(i)
            edge_out[way, 64:72, :] = places[:, tile(i)]
            pltpu.make_async_remote_copy(
                src_ref=edge_out.at[way],
                dst_ref=edge_in.at[way],
                send_sem=edge_send.at[way],
                recv_sem=edge_recv.at[way],
                device_id=(number // 8, number % 8),
                device_id_type=MESH,
            ).start()

    def boxes_of(k, at, first, count):
        return gathered[k].at[pl.ds(at[ORDERS[PARTS[k][0]][0]] * 32 + first, count)]

    def spread(k, first, count, step, sem):
        order, r0, c0, cols = PARTS[k]
        src = mult_ref.at[pl.ds(first, count), pl.ds(r0, ROWS), pl.ds(c0, cols)]
        dst = boxes_of(k, me, first, count)
        send(src, dst, g_send.at[k], g_recv.at[k, sem], moved(me, ORDERS[order][0], step), core)

    def pass_on(k):
        axis = ORDERS[PARTS[k][0]][0]
        for way, step in ((0, 3), (1, 1)):
            came = moved(me, axis, step)
            half = boxes_of(k, came, 16 * way, 16)
            drain(half, g_recv.at[k, way])
            send(half, half, g_send.at[k], g_recv.at[k, 2], moved(me, axis, 4 - step), core)

    for k in range(3):
        spread(k, 0, 16, 1, 0)
        spread(k, 16, 16, 3, 1)
    loads[2].wait()
    loads[3].wait()
    rows = 256
    down = lax.broadcasted_iota(jnp.int32, (rows, rows), 0)
    along = lax.broadcasted_iota(jnp.int32, (rows, rows), 1)
    across = jnp.concatenate([asked[0, 0:1, :], asked[0, 1:2, :]], 1)
    boxes_across = jnp.concatenate([asked[1, 0:1, :], asked[1, 1:2, :]], 1)
    owner = jnp.sum(jnp.where(down == along, across, 0), axis=1, keepdims=True)
    box = jnp.sum(jnp.where(down == along, boxes_across, 0), axis=1, keepdims=True)
    before = jnp.where((owner == across) & (along < down), 1, 0)
    rank = jnp.sum(before, axis=1, keepdims=True)
    row_rank = jnp.sum(jnp.where((owner == across) & (down < along), 1, 0), axis=0, keepdims=True)
    spots = {"x": across // 32, "z": across // 8 % 4, "y": across // 2 % 4}
    for order in range(3):
        g, p, q = (spots[axis] for axis in ORDERS[order])
        slot_v[order : order + 1, :] = ((p * 4 + q) * 2 + across % 2) * 8 + g * 2 + row_rank
    slot_v[3:8, :] = jnp.zeros((5, rows), jnp.int32)
    to_slots = pltpu.make_async_copy(slot_v, slot_s, copy_sem.at[1])
    to_slots.start()
    named = owner == lax.broadcasted_iota(jnp.int32, (rows, 128), 1)
    for r in range(2):
        wanted = jnp.sum(jnp.where(named & (rank == r), box, 0), axis=0, keepdims=True)
        ask_v[mine, r : r + 1, :] = wanted

    for step in (0, 1, 3, 2):
        for c in (core, 1 - core):
            if step == 0 and c is core:
                continue
            row = ask_v.at[pl.ds(mine, 1)]
            send(row, row, ask_send.at[0], ask_recv.at[0], moved(me, "y", step), c)

    for k in range(3):
        spread(k, 16, 16, 1, 2)
        spread(k, 0, 16, 3, 2)
    send_edges()
    drain(ask_v.at[pl.ds(0, 7)], ask_recv.at[0])
    for step in (1, 3, 2):
        part = ask_v.at[pl.ds(slab * 8, 8)]
        send(part, part, ask_send.at[1], ask_recv.at[1], moved(me, "z", step), core)
        send(part, part, ask_send.at[1], ask_recv.at[1], moved(me, "x", step), core)
    for z in (1, 3, 2):
        for x in (1, 3, 2):
            part = ask_v.at[pl.ds(slab * 8 + me["y"] * 2, 2)]
            send(part, part, ask_send.at[1], ask_recv.at[1], moved(moved(me, "z", z), "x", x), core)
    for k, (order, r0, c0, cols) in enumerate(PARTS):
        own_boxes = mult_ref.at[:, pl.ds(r0, ROWS), pl.ds(c0, cols)]
        pltpu.make_async_copy(own_boxes, boxes_of(k, me, 0, 32), g_own.at[k]).start()
    for k in range(3):
        pass_on(k)
    for k in range(3, 6):
        spread(k, 0, 16, 1, 0)
        spread(k, 16, 16, 3, 1)
        spread(k, 16, 16, 1, 2)
        spread(k, 0, 16, 3, 2)
    drain(ask_v.at[pl.ds(0, 66)], ask_recv.at[1])
    to_scalars = pltpu.make_async_copy(ask_v, ask_s, copy_sem.at[0])
    to_scalars.start()
    to_scalars.wait()

    def pack(k, steps):
        order, r0, c0, cols = PARTS[k]
        g, p, q = ORDERS[order]
        for step in steps:
            target = moved(me, p, step)

            def one(j, _):
                to = dict(target)
                to[q] = j // 8
                asker = index_of(to, (j // 4) % 2)
                source = dict(me)
                source[g] = j % 4
                served = index_of(source, core)
                for r in range(2):
                    row = ask_s[asker, r, served]
                    packed[k][target[p], 2 * j + r] = gathered[k][(j % 4) * 32 + row]
                return 0

            lax.fori_loop(0, 32, one, 0, unroll=4)
            if step:
                send(packed[k].at[target[p]], relay[k].at[me[p]], s_send.at[k], s_recv.at[k, me[p]], target, core)

    def boxes_are_here(k):
        drain(gathered[k].at[pl.ds(0, 64)], g_recv.at[k, 2])
        drain(gathered[k].at[pl.ds(0, 32)], g_own.at[k])

    def forward(k, step):
        order = PARTS[k][0]
        g, p, q = ORDERS[order]
        came = moved(me, p, step)
        src = packed[k] if step == 0 else relay[k]
        if step:
            drain(relay[k].at[came[p]], s_recv.at[k, came[p]])
        slot = ((came[p] * 4 + me[q]) * 2 + core) * 8
        for hop in (1, 3, 2, 0):
            for c in (core, 1 - core):
                to = moved(me, q, hop)
                piece = src.at[came[p], pl.ds((to[q] * 2 + c) * 8, 8)]
                dst = finals[k].at[pl.ds(slot, 8)]
                if hop == 0 and c is core:
                    pltpu.make_async_copy(piece, dst, f_own.at[k]).start()
                else:
                    send(piece, dst, f_send.at[k], f_recv.at[k], to, c)

    def near_sums():
        for way in range(2):
            drain(edge_in.at[way], edge_recv.at[way])
            drain(edge_out.at[way], edge_send.at[way])
        here = (mine > 0, mine < 127)
        for way in range(2):
            edge_in[way, 0:64, :] = jnp.where(here[way], edge_in[way, 0:64, :], 0.0)

        def half(i, before, now):
            joined = jnp.where(second, pltpu.roll(now, 64, 1), pltpu.roll(before, 64, 1))
            shifted[:, tile(i)] = joined[0:64].astype(jnp.bfloat16)
            columns[tile(i), 0:8] = jnp.transpose(joined[64:72])

        def own(i):
            return jnp.concatenate([masked(i), places[:, tile(i)]], 0)

        half(0, edge_in[0], own(0))
        half(16, own(15), edge_in[1])

        def middle(i, _):
            half(i, own(i - 1), own(i))
            return 0

        lax.fori_loop(1, 16, middle, 0)

        def pair(i, _):
            kernel_tiles = []
            for sb in range(4):
                o = jnp.where(second, sb - 2, sb - 1)
                at = columns[pl.ds(pl.multiple_of(i * 128 + sb * 64, 64), 64), 0:8]
                dx = places[0:1, tile(i)] - at[:, 0:1] - 2.0 * o.astype(jnp.float32)
                dy = places[1:2, tile(i)] - at[:, 1:2]
                dz = places[2:3, tile(i)] - at[:, 2:3]
                scaled = length_factor * jnp.sqrt(dx * dx + dy * dy + dz * dz)
                value = (1.0 + scaled) * jnp.exp(-scaled)
                kernel_tiles.append(jnp.where((o >= -1) & (o <= 1), value, 0.0))
            high, low = split(jnp.concatenate(kernel_tiles, 0))
            window = shifted[:, pl.ds(pl.multiple_of(i * 128, 128), 256)]
            potential_ref[:, tile(i)] = dot(window, high) + dot(window, low)
            return 0

        lax.fori_loop(0, 16, pair, 0)

    def weight_tables():
        node = lax.broadcasted_iota(jnp.int32, (8, 128), 0)
        factors = []
        for k in range(ORDER):
            column = jnp.zeros((8, 128), jnp.float32)
            for m in range(ORDER):
                column = jnp.where(node == m, math.cos(k * (2 * m + 1) * math.pi / (2 * ORDER)), column)
            factors.append(column)

        def pair(i, _):
            weights = []
            for axis in range(3):
                u = places[axis : axis + 1, tile(i)]
                old, new = jnp.ones_like(u), u
                value = factors[0] + factors[1] * u
                for k in range(2, ORDER):
                    old, new = new, 2.0 * u * new - old
                    value = value + factors[k] * new
                weights.append((2.0 * value - 1.0) / ORDER)
            for m1 in range(ORDER):
                parts = [(weights[0][m1 : m1 + 1] * weights[1][m2 : m2 + 1]) * weights[2] for m2 in range(ORDER)]
                high, low = split(jnp.concatenate(parts, 0))
                tables[i, m1 * 64 : m1 * 64 + 64, 0:128] = high
                tables[i, m1 * 64 : m1 * 64 + 64, 128:256] = low
            return 0

        lax.fori_loop(0, 16, pair, 0)

    def load_op(t):
        return pltpu.make_async_copy(
            ops_ref.at[t // 4, pl.ds(t % 4 * 512, 512)], stream.at[t % 2], stream_sem.at[t % 2]
        )

    def local_type(t):
        load_op(t).wait()
        if t + 1 < 16:
            load_op(t + 1).start()

        def group(i, _):
            for b in range(8):
                lhs[b * 64 : b * 64 + 64, 0:512] = mult[local_ref[t, i * 8 + b]]
            value = dot(lhs[:, 0:512], stream[t % 2]).reshape(8, 64, 512)
            if t == 0:
                total[pl.ds(i * 8, 8)] = value
            else:
                total[pl.ds(i * 8, 8)] += value
            return 0

        lax.fori_loop(0, 4, group, 0)

    def remote_rows(parts):
        r0 = PARTS[parts[0]][1]
        for k in parts:
            drain(finals[k].at[pl.ds(0, 224)], f_recv.at[k])
            drain(finals[k].at[pl.ds(0, 32)], f_own.at[k])

        def one(t, _):
            for k in parts:
                order, _, c0, cols = PARTS[k]
                for half in range(4):
                    for b in range(32):
                        at = pl.ds(half * 512 + c0, cols)
                        lhs[b * 16 : b * 16 + 16, at] = finals[k][slot_s[order, (4 * t + half) * 32 + b]]
            total[:, r0 : r0 + ROWS, :] += dot(lhs[...], ops[t]).reshape(32, ROWS, 512)
            return 0

        lax.fori_loop(0, 2, one, 0)

    def far_rows(r0, count):
        def pair(i, _):
            value = total[pl.ds(2 * i, 2), r0 : r0 + count, :].reshape(2 * count, 512)
            high, low = split(value)
            both = dot(jnp.concatenate([high, low], 0), tables[i])
            summed = (both[: 2 * count, 0:128] + both[: 2 * count, 128:256]) + (both[2 * count :, 0:128] + both[2 * count :, 128:256])
            far = jnp.where(second, summed[count:], summed[:count])
            near = potential_ref[r0 : r0 + count, tile(i)]
            potential_ref[r0 : r0 + count, tile(i)] = jnp.where(present(i), near + far, 0.0)
            return 0

        lax.fori_loop(0, 16, pair, 0, unroll=8)

    load_op(0).start()
    for k in range(3):
        boxes_are_here(k)
        pack(k, (2,))
    for k in range(3, 6):
        pass_on(k)
    for k in range(3):
        pack(k, (1, 3, 0))
    near_sums()
    weight_tables()
    loads[0].wait()
    loads[6].wait()
    for t in range(4):
        local_type(t)
    for k in range(3, 6):
        boxes_are_here(k)
        pack(k, (1, 3, 2, 0))
    t = 4
    for ks in ((0, 1, 2), (3, 4, 5)):
        for step in (0, 1, 3, 2):
            for k in ks:
                forward(k, step)
            if t < 16:
                local_type(t)
                local_type(t + 1)
                t += 2
    loads[7].wait()
    to_slots.wait()
    for k in range(3):
        remote_rows((k,))
    far_rows(0, 48)
    remote_rows((3, 4, 5))
    far_rows(48, 16)
    for k in range(6):
        drain(finals[k].at[pl.ds(0, 224)], f_send.at[k])
        drain(packed[k].at[pl.ds(0, 3)], s_send.at[k])
        drain(gathered[k].at[pl.ds(0, 96)], g_send.at[k])
    drain(ask_v.at[pl.ds(0, 7)], ask_send.at[0])
    drain(ask_v.at[pl.ds(0, 66)], ask_send.at[1])


def on_device(
    multipoles, translations, local_source, remote_owner, remote_box, charges, positions, leaf_count
):
    any_space = pl.BlockSpec(memory_space=pl.ANY)
    vmem = pl.BlockSpec(memory_space=pltpu.VMEM)
    dma = pltpu.SemaphoreType.DMA
    bf16, f32, i32 = jnp.bfloat16, jnp.float32, jnp.int32
    results = pl.pallas_call(
        whole_kernel,
        out_shape=[
            pltpu.VMEM((32, 64, 512), f32),
            pltpu.VMEM((64, 2048), f32),
        ]
        + [jax.ShapeDtypeStruct((4, 64, ROWS, part[3]), bf16) for part in PARTS],
        in_specs=[any_space] * 8,
        out_specs=[vmem, vmem] + [any_space] * 6,
        scratch_shapes=[pltpu.VMEM((128, ROWS, part[3]), bf16) for part in PARTS]
        + [pltpu.VMEM((4, 64, ROWS, part[3]), bf16) for part in PARTS]
        + [pltpu.VMEM((256, ROWS, part[3]), bf16) for part in PARTS]
        + [
            pltpu.VMEM((128, 2, 128), i32),
            pltpu.SMEM((128, 2, 128), i32),
            pltpu.VMEM((8, 256), i32),
            pltpu.SMEM((8, 256), i32),
            pltpu.VMEM((32, 64, 512), bf16),
            pltpu.VMEM((2, 2048, 512), bf16),
            pltpu.VMEM((2, 512, 512), bf16),
            pltpu.VMEM((512, 2048), bf16),
            pltpu.VMEM((64, 2048), bf16),
            pltpu.VMEM((8, 2048), f32),
            pltpu.VMEM((64, 2176), bf16),
            pltpu.VMEM((2176, 8), f32),
            pltpu.VMEM((16, 512, 256), bf16),
            pltpu.VMEM((2, 72, 128), f32),
            pltpu.VMEM((2, 72, 128), f32),
            pltpu.VMEM((2, 2, 128), i32),
            pltpu.SMEM((16, 32), i32),
            pltpu.SMEM((32,), i32),
            dma((2,)), dma((2,)), dma((2,)), dma((6,)), dma((6, 3)), dma((6,)), dma((6,)), dma((6, 4)), dma((6,)), dma((6,)), dma((6,)),
            dma((8,)), dma((2,)), dma((2,)), dma((2,)),
        ],
        compiler_params=pltpu.CompilerParams(collective_id=0, has_side_effects=True, vmem_limit_bytes=57 * 2**20),
    )(remote_owner.reshape(2, 128), remote_box.reshape(2, 128), local_source, leaf_count, multipoles, translations.reshape(6, 2048, 512), charges, positions)
    return results[0], results[1]


def solution(mesh):
    placed = (
        P(("slab", "sub"), None, None),
        P(),
        P(None, ("slab", "sub")),
        P(("slab", "sub"), None),
        P(("slab", "sub")),
        P(None, ("slab", "sub")),
        P(None, ("slab", "sub")),
        P(("slab", "sub")),
    )
    return jax.shard_map(
        on_device,
        mesh=mesh,
        in_specs=placed,
        out_specs=(P(("slab", "sub"), None, None), P(None, ("slab", "sub"))),
        check_vma=False,
    )
```

```python
import math

import jax
import jax.numpy as jnp
from jax import lax
from jax.experimental import pallas as pl
from jax.experimental.pallas import tpu as pltpu
from jax.sharding import PartitionSpec as P

ORDER = 8
SLOTS = 64
length_factor = 1.7320508075688772
MESH = pl.DeviceIdType.MESH

PARTS = ((0, 0, 0, 512), (1, 16, 0, 512), (2, 32, 0, 512), (0, 48, 0, 128), (1, 48, 128, 128), (2, 48, 256, 256))
STARTS = (0, 512, 1024)
ORDERS = ("xyz", "yzx", "zxy")
ROWS = 16


def place(at, core):
    return (at["x"] * 4 + at["z"], at["y"] * 2 + core)


def index_of(at, core):
    return at["x"] * 32 + at["z"] * 8 + at["y"] * 2 + core


def moved(at, axis, step):
    other = dict(at)
    other[axis] = (at[axis] + step) % 4
    return other


def dot(a, b):
    return jnp.dot(a, b, preferred_element_type=jnp.float32)


def split(value):
    high = value.astype(jnp.bfloat16)
    return high, (value - high.astype(jnp.float32)).astype(jnp.bfloat16)


def add_far(values, r0, count, tables, potentials):
    def pair(i, _):
        value = values[pl.ds(2 * i, 2), r0 : r0 + count, :].reshape(2 * count, 512)
        high, low = split(value)
        both = dot(jnp.concatenate([high, low], 0), tables[i])
        summed = (both[: 2 * count, 0:128] + both[: 2 * count, 128:256]) + (
            both[2 * count :, 0:128] + both[2 * count :, 128:256]
        )
        second = lax.broadcasted_iota(jnp.int32, (1, 128), 1) >= 64
        at = pl.ds(pl.multiple_of(i * 128, 128), 128)
        potentials[0:count, at] += jnp.where(second, summed[count:], summed[:count])
        return 0

    lax.fori_loop(0, 16, pair, 0, unroll=8)


def whole_kernel(
    owner_ref, box_ref, local_hbm, count_hbm, mult_ref, ops_ref, charge_ref, pos_ref, expansion_ref, potential_ref, *scratch
):
    tables, ops, last = scratch[0:3]
    relay, scratch = scratch[3:9], scratch[9:]
    gathered, packed, finals = scratch[0:6], scratch[6:12], scratch[12:18]
    ask_v, ask_s, slot_v, slot_s = scratch[18:22]
    mult, stream, lhs, charges, places, shifted, columns, edge_out, edge_in = scratch[22:31]
    asked, local_ref, count_ref = scratch[31:34]
    total = expansion_ref
    (ask_send, ask_recv, copy_sem, g_send, g_recv, g_own, s_send, s_recv, f_send, f_recv, f_own) = scratch[34:45]
    load_sem, stream_sem, edge_send, edge_recv = scratch[45:]
    slab, sub = lax.axis_index("slab"), lax.axis_index("sub")
    me = {"x": slab // 4, "y": sub // 2, "z": slab % 4}
    core = sub % 2
    mine = index_of(me, core)

    barrier = pltpu.get_barrier_semaphore()
    partners = [(me, 1 - core)]
    for axis in "xyz":
        for step in (1, 3, 2):
            for other in (core, 1 - core):
                partners.append((moved(me, axis, step), other))
    for z in (1, 3, 2):
        for x in (1, 3, 2):
            partners.append((moved(moved(me, "z", z), "x", x), core))
    for at, c in partners:
        pl.semaphore_signal(barrier, 1, device_id=place(at, c), device_id_type=MESH)
    after, prior = (mine + 1) % 128, (mine + 127) % 128
    for number in (after, prior):
        pl.semaphore_signal(barrier, 1, device_id=(number // 8, number % 8), device_id_type=MESH)

    pl.semaphore_wait(barrier, len(partners) + 2)

    def send(src, dst, ssem, rsem, at, c):
        pltpu.make_async_remote_copy(
            src_ref=src, dst_ref=dst, send_sem=ssem, recv_sem=rsem, device_id=place(at, c), device_id_type=MESH
        ).start()

    def drain(ref, sem):
        pltpu.make_async_copy(ref, ref, sem).wait()

    lane = lax.broadcasted_iota(jnp.int32, (1, 128), 1)
    second = lane >= 64

    def tile(i):
        return pl.ds(pl.multiple_of(i * 128, 128), 128)

    def present(i):
        return (lane % 64) < jnp.where(second, count_ref[2 * i + 1], count_ref[2 * i])

    def masked(i):
        return jnp.where(present(i), charges[:, tile(i)].astype(jnp.float32), 0.0)

    def send_edges():
        loads[1].wait()
        loads[4].wait()
        loads[5].wait()
        for way, (i, number) in enumerate(((15, after), (0, prior))):
            edge_out[way, 0:64, :] = masked(i)
            edge_out[way, 64:72, :] = places[:, tile(i)]
            pltpu.make_async_remote_copy(
                src_ref=edge_out.at[way],
                dst_ref=edge_in.at[way],
                send_sem=edge_send.at[way],
                recv_sem=edge_recv.at[way],
                device_id=(number // 8, number % 8),
                device_id_type=MESH,
            ).start()

    def boxes_of(k, at, first, count):
        return gathered[k].at[pl.ds(at[ORDERS[PARTS[k][0]][0]] * 32 + first, count)]

    def spread(k, first, count, step, sem):
        order, r0, c0, cols = PARTS[k]
        src = mult_ref.at[pl.ds(first, count), pl.ds(r0, ROWS), pl.ds(c0, cols)]
        dst = boxes_of(k, me, first, count)
        send(src, dst, g_send.at[k], g_recv.at[k, sem], moved(me, ORDERS[order][0], step), core)

    def pass_on(k):
        axis = ORDERS[PARTS[k][0]][0]
        for way, step in ((0, 3), (1, 1)):
            came = moved(me, axis, step)
            half = boxes_of(k, came, 16 * way, 16)
            drain(half, g_recv.at[k, way])
            send(half, half, g_send.at[k], g_recv.at[k, 2], moved(me, axis, 4 - step), core)

    for k in range(3):
        spread(k, 0, 16, 1, 0)
        spread(k, 16, 16, 3, 1)
    loads = [
        pltpu.make_async_copy(local_hbm, local_ref, load_sem.at[4]),
        pltpu.make_async_copy(count_hbm, count_ref, load_sem.at[5]),
        pltpu.make_async_copy(owner_ref, asked.at[0], load_sem.at[6]),
        pltpu.make_async_copy(box_ref, asked.at[1], load_sem.at[7]),
        pltpu.make_async_copy(charge_ref, charges, load_sem.at[0]),
        pltpu.make_async_copy(pos_ref, places.at[pl.ds(0, 3)], load_sem.at[1]),
        pltpu.make_async_copy(mult_ref, mult, load_sem.at[2]),
    ]
    places[...] = jnp.zeros_like(places)
    for load in loads:
        load.start()
    for t in range(8):
        for (_, _, c0, cols), start in zip(PARTS[3:], STARTS):
            pltpu.make_async_copy(
                ops_ref.at[16 + t, pl.ds(c0, cols)], ops.at[t // 4, pl.ds(start + t % 4 * cols, cols)], load_sem.at[3]
            ).start()
    loads[2].wait()
    loads[3].wait()
    rows = 256
    down = lax.broadcasted_iota(jnp.int32, (rows, rows), 0)
    along = lax.broadcasted_iota(jnp.int32, (rows, rows), 1)
    across = jnp.concatenate([asked[0, 0:1, :], asked[0, 1:2, :]], 1)
    boxes_across = jnp.concatenate([asked[1, 0:1, :], asked[1, 1:2, :]], 1)
    owner = jnp.sum(jnp.where(down == along, across, 0), axis=1, keepdims=True)
    box = jnp.sum(jnp.where(down == along, boxes_across, 0), axis=1, keepdims=True)
    before = jnp.where((owner == across) & (along < down), 1, 0)
    rank = jnp.sum(before, axis=1, keepdims=True)
    row_rank = jnp.sum(jnp.where((owner == across) & (down < along), 1, 0), axis=0, keepdims=True)
    spots = {"x": across // 32, "z": across // 8 % 4, "y": across // 2 % 4}
    for order in range(3):
        g, p, q = (spots[axis] for axis in ORDERS[order])
        slot_v[order : order + 1, :] = ((p * 4 + q) * 2 + across % 2) * 8 + g * 2 + row_rank
    slot_v[3:8, :] = jnp.zeros((5, rows), jnp.int32)
    to_slots = pltpu.make_async_copy(slot_v, slot_s, copy_sem.at[1])
    to_slots.start()
    named = owner == lax.broadcasted_iota(jnp.int32, (rows, 128), 1)
    for r in range(2):
        wanted = jnp.sum(jnp.where(named & (rank == r), box, 0), axis=0, keepdims=True)
        ask_v[mine, r : r + 1, :] = wanted

    for step in (0, 1, 3, 2):
        for c in (core, 1 - core):
            if step == 0 and c is core:
                continue
            row = ask_v.at[pl.ds(mine, 1)]
            send(row, row, ask_send.at[0], ask_recv.at[0], moved(me, "y", step), c)

    for k in range(3):
        spread(k, 16, 16, 1, 2)
        spread(k, 0, 16, 3, 2)
    send_edges()
    drain(ask_v.at[pl.ds(0, 7)], ask_recv.at[0])
    for step in (1, 3, 2):
        part = ask_v.at[pl.ds(slab * 8, 8)]
        send(part, part, ask_send.at[1], ask_recv.at[1], moved(me, "z", step), core)
        send(part, part, ask_send.at[1], ask_recv.at[1], moved(me, "x", step), core)
    for z in (1, 3, 2):
        for x in (1, 3, 2):
            part = ask_v.at[pl.ds(slab * 8 + me["y"] * 2, 2)]
            send(part, part, ask_send.at[1], ask_recv.at[1], moved(moved(me, "z", z), "x", x), core)
    for k, (order, r0, c0, cols) in enumerate(PARTS):
        own_boxes = mult_ref.at[:, pl.ds(r0, ROWS), pl.ds(c0, cols)]
        pltpu.make_async_copy(own_boxes, boxes_of(k, me, 0, 32), g_own.at[k]).start()
    for k in range(3):
        pass_on(k)
    for k in range(3, 6):
        spread(k, 0, 16, 1, 0)
        spread(k, 16, 16, 3, 1)
        spread(k, 16, 16, 1, 2)
        spread(k, 0, 16, 3, 2)
    drain(ask_v.at[pl.ds(0, 66)], ask_recv.at[1])
    to_scalars = pltpu.make_async_copy(ask_v, ask_s, copy_sem.at[0])
    to_scalars.start()
    to_scalars.wait()

    def pack(k, steps):
        order, r0, c0, cols = PARTS[k]
        g, p, q = ORDERS[order]
        for step in steps:
            target = moved(me, p, step)

            def one(j, _):
                to = dict(target)
                to[q] = j // 8
                asker = index_of(to, (j // 4) % 2)
                source = dict(me)
                source[g] = j % 4
                served = index_of(source, core)
                for r in range(2):
                    row = ask_s[asker, r, served]
                    packed[k][target[p], 2 * j + r] = gathered[k][(j % 4) * 32 + row]
                return 0

            lax.fori_loop(0, 32, one, 0, unroll=4)
            if step:
                send(packed[k].at[target[p]], relay[k].at[me[p]], s_send.at[k], s_recv.at[k, me[p]], target, core)

    def boxes_are_here(k):
        drain(gathered[k].at[pl.ds(0, 64)], g_recv.at[k, 2])
        drain(gathered[k].at[pl.ds(0, 32)], g_own.at[k])

    def forward(k, step):
        order = PARTS[k][0]
        g, p, q = ORDERS[order]
        came = moved(me, p, step)
        src = packed[k] if step == 0 else relay[k]
        if step:
            drain(relay[k].at[came[p]], s_recv.at[k, came[p]])
        slot = ((came[p] * 4 + me[q]) * 2 + core) * 8
        for hop in (1, 3, 2, 0):
            for c in (core, 1 - core):
                to = moved(me, q, hop)
                piece = src.at[came[p], pl.ds((to[q] * 2 + c) * 8, 8)]
                dst = finals[k].at[pl.ds(slot, 8)]
                if hop == 0 and c is core:
                    pltpu.make_async_copy(piece, dst, f_own.at[k]).start()
                else:
                    send(piece, dst, f_send.at[k], f_recv.at[k], to, c)

    def near_sums():
        for way in range(2):
            drain(edge_in.at[way], edge_recv.at[way])
            drain(edge_out.at[way], edge_send.at[way])
        here = (mine > 0, mine < 127)
        for way in range(2):
            edge_in[way, 0:64, :] = jnp.where(here[way], edge_in[way, 0:64, :], 0.0)

        def half(i, before, now):
            joined = jnp.where(second, pltpu.roll(now, 64, 1), pltpu.roll(before, 64, 1))
            shifted[:, tile(i)] = joined[0:64].astype(jnp.bfloat16)
            columns[tile(i), 0:8] = jnp.transpose(joined[64:72])

        def own(i):
            return jnp.concatenate([masked(i), places[:, tile(i)]], 0)

        half(0, edge_in[0], own(0))
        half(16, own(15), edge_in[1])

        def middle(i, _):
            half(i, own(i - 1), own(i))
            return 0

        lax.fori_loop(1, 16, middle, 0)

        def pair(i, _):
            kernel_tiles = []
            for sb in range(4):
                o = jnp.where(second, sb - 2, sb - 1)
                at = columns[pl.ds(pl.multiple_of(i * 128 + sb * 64, 64), 64), 0:8]
                dx = places[0:1, tile(i)] - at[:, 0:1] - 2.0 * o.astype(jnp.float32)
                dy = places[1:2, tile(i)] - at[:, 1:2]
                dz = places[2:3, tile(i)] - at[:, 2:3]
                scaled = length_factor * jnp.sqrt(dx * dx + dy * dy + dz * dz)
                value = (1.0 + scaled) * jnp.exp(-scaled)
                kernel_tiles.append(jnp.where((o >= -1) & (o <= 1), value, 0.0))
            high, low = split(jnp.concatenate(kernel_tiles, 0))
            window = shifted[:, pl.ds(pl.multiple_of(i * 128, 128), 256)]
            potential_ref[:, tile(i)] = jnp.where(present(i), dot(window, high) + dot(window, low), 0.0)
            return 0

        lax.fori_loop(0, 16, pair, 0)

    def weight_tables():
        node = lax.broadcasted_iota(jnp.int32, (8, 128), 0)
        factors = []
        for k in range(ORDER):
            column = jnp.zeros((8, 128), jnp.float32)
            for m in range(ORDER):
                column = jnp.where(node == m, math.cos(k * (2 * m + 1) * math.pi / (2 * ORDER)), column)
            factors.append(column)

        def pair(i, _):
            weights = []
            for axis in range(3):
                u = places[axis : axis + 1, tile(i)]
                old, new = jnp.ones_like(u), u
                value = factors[0] + factors[1] * u
                for k in range(2, ORDER):
                    old, new = new, 2.0 * u * new - old
                    value = value + factors[k] * new
                weights.append((2.0 * value - 1.0) / ORDER)
            weights[2] = jnp.where(present(i), weights[2], 0.0)
            for m1 in range(ORDER):
                parts = [(weights[0][m1 : m1 + 1] * weights[1][m2 : m2 + 1]) * weights[2] for m2 in range(ORDER)]
                high, low = split(jnp.concatenate(parts, 0))
                tables[i, m1 * 64 : m1 * 64 + 64, 0:128] = high
                tables[i, m1 * 64 : m1 * 64 + 64, 128:256] = low
            return 0

        lax.fori_loop(0, 16, pair, 0)

    def load_op(t):
        return pltpu.make_async_copy(
            ops_ref.at[t], stream.at[t % 2], stream_sem.at[t % 2]
        )

    def local_type(t):
        load_op(t).wait()
        if t + 1 < 16:
            load_op(t + 1).start()

        def group(i, _):
            for b in range(8):
                lhs[b * 64 : b * 64 + 64, 0:512] = mult[local_ref[t, i * 8 + b]]
            value = dot(lhs[:, 0:512], stream[t % 2]).reshape(8, 64, 512)
            if t == 0:
                total[pl.ds(i * 8, 8)] = value
            else:
                total[pl.ds(i * 8, 8)] += value
            return 0

        lax.fori_loop(0, 4, group, 0)

    def arrived(k):
        drain(finals[k].at[pl.ds(0, 224)], f_recv.at[k])
        drain(finals[k].at[pl.ds(0, 32)], f_own.at[k])

    def remote_rows(k):
        order, r0, _, _ = PARTS[k]
        arrived(k)

        def one(half, _):
            for t in range(4):
                for b in range(32):
                    block = finals[k][slot_s[order, (4 * half + t) * 32 + b]]
                    for (_, _, c0, cols), start in zip(PARTS[3:], STARTS):
                        lhs[b * 16 : b * 16 + 16, start + t * cols : start + (t + 1) * cols] = block[:, c0 : c0 + cols]
            total[:, r0 : r0 + ROWS, :] += dot(lhs[...], ops[half]).reshape(32, ROWS, 512)
            return 0

        lax.fori_loop(0, 2, one, 0)

    def fetch(k, half, t, b):
        return finals[k][slot_s[PARTS[k][0], (4 * half + t) * 32 + b]]

    def add_last(value):
        total[:, 48:64, :] += value.reshape(32, ROWS, 512)

    def last_rows_first_part():
        arrived(3)

        def one(half, _):
            for t in range(4):
                for b in range(32):
                    lhs[b * 16 : b * 16 + 16, t * 128 : t * 128 + 128] = fetch(3, half, t, b)
            add_last(dot(lhs[:, 0:512], ops[half, 0:512]))
            return 0

        lax.fori_loop(0, 2, one, 0)

    def last_rows_other_parts():
        arrived(4)
        arrived(5)
        for half in range(2):
            for t in range(4):
                for b in range(32):
                    rows16, at = slice(b * 16, b * 16 + 16), half * 1536 + t * 128
                    last[rows16, at : at + 128] = fetch(4, half, t, b)
                    at = half * 1536 + 512 + t * 256
                    last[rows16, at : at + 256] = fetch(5, half, t, b)

    load_op(0).start()
    for k in range(3):
        boxes_are_here(k)
        pack(k, (2,))
    for k in range(3, 6):
        pass_on(k)
    for k in range(3):
        pack(k, (1, 3, 0))
    near_sums()
    weight_tables()
    loads[0].wait()
    loads[6].wait()
    for t in range(4):
        local_type(t)
    for k in range(3, 6):
        boxes_are_here(k)
        pack(k, (1, 3, 2, 0))
    t = 4
    for ks in ((0, 1, 2), (3, 4, 5)):
        for step in (0, 2, 1, 3):
            for k in ks:
                forward(k, step)
            if t < 16:
                local_type(t)
                local_type(t + 1)
                t += 2
    drain(ops, load_sem.at[3])
    to_slots.wait()
    for k in range(3):
        remote_rows(k)
    add_far(total, 0, 48, tables, potential_ref)
    last_rows_first_part()
    last_rows_other_parts()
    for k in range(6):
        drain(finals[k].at[pl.ds(0, 224)], f_send.at[k])
        drain(packed[k].at[pl.ds(0, 3)], s_send.at[k])
        drain(gathered[k].at[pl.ds(0, 96)], g_send.at[k])
    drain(ask_v.at[pl.ds(0, 7)], ask_send.at[0])
    drain(ask_v.at[pl.ds(0, 66)], ask_send.at[1])


def finish_kernel(
    expansion_ref, potential_ref, tables, ops, last, expansion_out, potential_out, rows, potentials, sems
):
    copies = [
        pltpu.make_async_copy(
            expansion_ref.at[pl.ds(i * 8, 8), pl.ds(0, 48)], expansion_out.at[pl.ds(i * 8, 8), pl.ds(0, 48)], sems.at[i]
        )
        for i in range(4)
    ]
    copies.append(pltpu.make_async_copy(potential_ref.at[pl.ds(0, 48)], potential_out.at[pl.ds(0, 48)], sems.at[4]))
    for copy in copies:
        copy.start()
    value = dot(last[:, 0:1536], ops[0, 512:2048]) + dot(last[:, 1536:3072], ops[1, 512:2048])
    rows[...] = expansion_ref[:, 48:64, :] + value.reshape(32, ROWS, 512)
    copies.append(pltpu.make_async_copy(rows, expansion_out.at[:, pl.ds(48, 16)], sems.at[5]))
    copies[-1].start()
    potentials[...] = potential_ref[48:64, :]
    add_far(rows, 0, ROWS, tables, potentials)
    copies.append(pltpu.make_async_copy(potentials, potential_out.at[pl.ds(48, 16)], sems.at[6]))
    copies[-1].start()
    for copy in copies:
        copy.wait()


def on_device(
    multipoles, translations, local_source, remote_owner, remote_box, charges, positions, leaf_count
):
    any_space = pl.BlockSpec(memory_space=pl.ANY)
    vmem = pl.BlockSpec(memory_space=pltpu.VMEM)
    dma = pltpu.SemaphoreType.DMA
    bf16, f32, i32 = jnp.bfloat16, jnp.float32, jnp.int32
    results = pl.pallas_call(
        whole_kernel,
        out_shape=[
            pltpu.VMEM((32, 64, 512), f32),
            pltpu.VMEM((64, 2048), f32),
            pltpu.VMEM((16, 512, 256), bf16),
            pltpu.VMEM((2, 2048, 512), bf16),
            pltpu.VMEM((512, 3072), bf16),
        ]
        + [jax.ShapeDtypeStruct((4, 64, ROWS, part[3]), bf16) for part in PARTS],
        in_specs=[any_space] * 8,
        out_specs=[vmem] * 5 + [any_space] * 6,
        scratch_shapes=[pltpu.VMEM((128, ROWS, part[3]), bf16) for part in PARTS]
        + [pltpu.VMEM((4, 64, ROWS, part[3]), bf16) for part in PARTS]
        + [pltpu.VMEM((256, ROWS, part[3]), bf16) for part in PARTS]
        + [
            pltpu.VMEM((128, 2, 128), i32),
            pltpu.SMEM((128, 2, 128), i32),
            pltpu.VMEM((8, 256), i32),
            pltpu.SMEM((8, 256), i32),
            pltpu.VMEM((32, 64, 512), bf16),
            pltpu.VMEM((2, 512, 512), bf16),
            pltpu.VMEM((512, 2048), bf16),
            pltpu.VMEM((64, 2048), bf16),
            pltpu.VMEM((8, 2048), f32),
            pltpu.VMEM((64, 2176), bf16),
            pltpu.VMEM((2176, 8), f32),
            pltpu.VMEM((2, 72, 128), f32),
            pltpu.VMEM((2, 72, 128), f32),
            pltpu.VMEM((2, 2, 128), i32),
            pltpu.SMEM((16, 32), i32),
            pltpu.SMEM((32,), i32),
            dma((2,)), dma((2,)), dma((2,)), dma((6,)), dma((6, 3)), dma((6,)), dma((6,)), dma((6, 4)), dma((6,)), dma((6,)), dma((6,)),
            dma((8,)), dma((2,)), dma((2,)), dma((2,)),
        ],
        compiler_params=pltpu.CompilerParams(collective_id=0, has_side_effects=True, vmem_limit_bytes=48 * 2**20),
    )(remote_owner.reshape(2, 128), remote_box.reshape(2, 128), local_source, leaf_count, multipoles, translations, charges, positions)
    held = [pltpu.with_memory_space_constraint(value, pltpu.VMEM) for value in results[:5]]
    return pl.pallas_call(
        finish_kernel,
        out_shape=[jax.ShapeDtypeStruct((32, 64, 512), f32), jax.ShapeDtypeStruct((64, 2048), f32)],
        in_specs=[vmem] * 5,
        out_specs=[any_space] * 2,
        scratch_shapes=[pltpu.VMEM((32, ROWS, 512), f32), pltpu.VMEM((ROWS, 2048), f32), dma((7,))],
        compiler_params=pltpu.CompilerParams(vmem_limit_bytes=4 * 2**20),
    )(*held)


def solution(mesh):
    placed = (
        P(("slab", "sub"), None, None),
        P(),
        P(None, ("slab", "sub")),
        P(("slab", "sub"), None),
        P(("slab", "sub")),
        P(None, ("slab", "sub")),
        P(None, ("slab", "sub")),
        P(("slab", "sub")),
    )
    return jax.shard_map(
        on_device,
        mesh=mesh,
        in_specs=placed,
        out_specs=(P(("slab", "sub"), None, None), P(None, ("slab", "sub"))),
        check_vma=False,
    )
```

```python
import math

import jax
import jax.numpy as jnp
from jax import lax
from jax.experimental import pallas as pl
from jax.experimental.pallas import tpu as pltpu
from jax.sharding import PartitionSpec as P

ORDER = 8
SLOTS = 64
length_factor = 1.7320508075688772
MESH = pl.DeviceIdType.MESH

PARTS = ((0, 0, 0, 512), (1, 16, 0, 512), (2, 32, 0, 512), (0, 48, 0, 128), (1, 48, 128, 128), (2, 48, 256, 256))
STARTS = (0, 512, 1024)
ORDERS = ("xyz", "yzx", "zxy")
ROWS = 16


def place(at, core):
    return (at["x"] * 4 + at["z"], at["y"] * 2 + core)


def index_of(at, core):
    return at["x"] * 32 + at["z"] * 8 + at["y"] * 2 + core


def moved(at, axis, step):
    other = dict(at)
    other[axis] = (at[axis] + step) % 4
    return other


def dot(a, b):
    return jnp.dot(a, b, preferred_element_type=jnp.float32)


def split(value):
    high = value.astype(jnp.bfloat16)
    return high, (value - high.astype(jnp.float32)).astype(jnp.bfloat16)


def add_far(values, r0, count, tables, potentials):
    def pair(i, _):
        value = values[pl.ds(2 * i, 2), r0 : r0 + count, :].reshape(2 * count, 512)
        high, low = split(value)
        both = dot(jnp.concatenate([high, low], 0), tables[i])
        summed = (both[: 2 * count, 0:128] + both[: 2 * count, 128:256]) + (
            both[2 * count :, 0:128] + both[2 * count :, 128:256]
        )
        second = lax.broadcasted_iota(jnp.int32, (1, 128), 1) >= 64
        at = pl.ds(pl.multiple_of(i * 128, 128), 128)
        potentials[0:count, at] += jnp.where(second, summed[count:], summed[:count])
        return 0

    lax.fori_loop(0, 16, pair, 0, unroll=8)


def whole_kernel(
    owner_ref, box_ref, local_hbm, count_hbm, mult_ref, ops_ref, charge_ref, pos_ref, expansion_ref, potential_ref, *scratch
):
    tables, ops, last = scratch[0:3]
    relay, scratch = scratch[3:9], scratch[9:]
    gathered, packed, finals = scratch[0:6], scratch[6:12], scratch[12:18]
    ask_v, ask_s, slot_v, slot_s = scratch[18:22]
    mult, stream, lhs, charges, places, shifted, columns, edge_out, edge_in = scratch[22:31]
    asked, local_ref, count_ref = scratch[31:34]
    total = expansion_ref
    (ask_send, ask_recv, copy_sem, g_send, g_recv, g_own, s_send, s_recv, f_send, f_recv, f_own) = scratch[34:45]
    load_sem, stream_sem, edge_send, edge_recv = scratch[45:]
    slab, sub = lax.axis_index("slab"), lax.axis_index("sub")
    me = {"x": slab // 4, "y": sub // 2, "z": slab % 4}
    core = sub % 2
    mine = index_of(me, core)

    barrier = pltpu.get_barrier_semaphore()
    partners = [(me, 1 - core)]
    for axis in "xyz":
        for step in (1, 3, 2):
            for other in (core, 1 - core):
                partners.append((moved(me, axis, step), other))
    for z in (1, 3, 2):
        for x in (1, 3, 2):
            partners.append((moved(moved(me, "z", z), "x", x), core))
    for at, c in partners:
        pl.semaphore_signal(barrier, 1, device_id=place(at, c), device_id_type=MESH)
    after, prior = (mine + 1) % 128, (mine + 127) % 128
    for number in (after, prior):
        pl.semaphore_signal(barrier, 1, device_id=(number // 8, number % 8), device_id_type=MESH)

    pl.semaphore_wait(barrier, len(partners) + 2)

    def send(src, dst, ssem, rsem, at, c):
        pltpu.make_async_remote_copy(
            src_ref=src, dst_ref=dst, send_sem=ssem, recv_sem=rsem, device_id=place(at, c), device_id_type=MESH
        ).start()

    def drain(ref, sem):
        pltpu.make_async_copy(ref, ref, sem).wait()

    lane = lax.broadcasted_iota(jnp.int32, (1, 128), 1)
    second = lane >= 64

    def tile(i):
        return pl.ds(pl.multiple_of(i * 128, 128), 128)

    def present(i):
        return (lane % 64) < jnp.where(second, count_ref[2 * i + 1], count_ref[2 * i])

    def masked(i):
        return jnp.where(present(i), charges[:, tile(i)].astype(jnp.float32), 0.0)

    def send_edges():
        loads[1].wait()
        loads[4].wait()
        loads[5].wait()
        for way, (i, number) in enumerate(((15, after), (0, prior))):
            edge_out[way, 0:64, :] = masked(i)
            edge_out[way, 64:72, :] = places[:, tile(i)]
            pltpu.make_async_remote_copy(
                src_ref=edge_out.at[way],
                dst_ref=edge_in.at[way],
                send_sem=edge_send.at[way],
                recv_sem=edge_recv.at[way],
                device_id=(number // 8, number % 8),
                device_id_type=MESH,
            ).start()

    def boxes_of(k, at, first, count):
        return gathered[k].at[pl.ds(at[ORDERS[PARTS[k][0]][0]] * 32 + first, count)]

    def spread(k, first, count, step, sem):
        order, r0, c0, cols = PARTS[k]
        src = mult_ref.at[pl.ds(first, count), pl.ds(r0, ROWS), pl.ds(c0, cols)]
        dst = boxes_of(k, me, first, count)
        send(src, dst, g_send.at[k], g_recv.at[k, sem], moved(me, ORDERS[order][0], step), core)

    def pass_on(k):
        axis = ORDERS[PARTS[k][0]][0]
        for way, step in ((0, 3), (1, 1)):
            came = moved(me, axis, step)
            half = boxes_of(k, came, 16 * way, 16)
            drain(half, g_recv.at[k, way])
            send(half, half, g_send.at[k], g_recv.at[k, 2], moved(me, axis, 4 - step), core)

    for k in range(3):
        spread(k, 0, 16, 1, 0)
        spread(k, 16, 16, 3, 1)
    loads = [
        pltpu.make_async_copy(local_hbm, local_ref, load_sem.at[4]),
        pltpu.make_async_copy(count_hbm, count_ref, load_sem.at[5]),
        pltpu.make_async_copy(owner_ref, asked.at[0], load_sem.at[6]),
        pltpu.make_async_copy(box_ref, asked.at[1], load_sem.at[7]),
        pltpu.make_async_copy(charge_ref, charges, load_sem.at[0]),
        pltpu.make_async_copy(pos_ref, places.at[pl.ds(0, 3)], load_sem.at[1]),
        pltpu.make_async_copy(mult_ref, mult, load_sem.at[2]),
    ]
    places[...] = jnp.zeros_like(places)
    for load in loads:
        load.start()
    for t in range(8):
        for (_, _, c0, cols), start in zip(PARTS[3:], STARTS):
            pltpu.make_async_copy(
                ops_ref.at[16 + t, pl.ds(c0, cols)], ops.at[t // 4, pl.ds(start + t % 4 * cols, cols)], load_sem.at[3]
            ).start()
    loads[2].wait()
    loads[3].wait()
    rows = 256
    down = lax.broadcasted_iota(jnp.int32, (rows, rows), 0)
    along = lax.broadcasted_iota(jnp.int32, (rows, rows), 1)
    across = jnp.concatenate([asked[0, 0:1, :], asked[0, 1:2, :]], 1)
    boxes_across = jnp.concatenate([asked[1, 0:1, :], asked[1, 1:2, :]], 1)
    owner = jnp.sum(jnp.where(down == along, across, 0), axis=1, keepdims=True)
    box = jnp.sum(jnp.where(down == along, boxes_across, 0), axis=1, keepdims=True)
    before = jnp.where((owner == across) & (along < down), 1, 0)
    rank = jnp.sum(before, axis=1, keepdims=True)
    row_rank = jnp.sum(jnp.where((owner == across) & (down < along), 1, 0), axis=0, keepdims=True)
    spots = {"x": across // 32, "z": across // 8 % 4, "y": across // 2 % 4}
    for order in range(3):
        g, p, q = (spots[axis] for axis in ORDERS[order])
        slot_v[order : order + 1, :] = ((p * 4 + q) * 2 + across % 2) * 8 + g * 2 + row_rank
    slot_v[3:8, :] = jnp.zeros((5, rows), jnp.int32)
    to_slots = pltpu.make_async_copy(slot_v, slot_s, copy_sem.at[1])
    to_slots.start()
    named = owner == lax.broadcasted_iota(jnp.int32, (rows, 128), 1)
    for r in range(2):
        wanted = jnp.sum(jnp.where(named & (rank == r), box, 0), axis=0, keepdims=True)
        ask_v[mine, r : r + 1, :] = wanted

    for step in (0, 1, 3, 2):
        for c in (core, 1 - core):
            if step == 0 and c is core:
                continue
            row = ask_v.at[pl.ds(mine, 1)]
            send(row, row, ask_send.at[0], ask_recv.at[0], moved(me, "y", step), c)

    for k in range(3):
        spread(k, 16, 16, 1, 2)
        spread(k, 0, 16, 3, 2)
    send_edges()
    drain(ask_v.at[pl.ds(0, 7)], ask_recv.at[0])
    for step in (1, 3, 2):
        part = ask_v.at[pl.ds(slab * 8, 8)]
        send(part, part, ask_send.at[1], ask_recv.at[1], moved(me, "z", step), core)
        send(part, part, ask_send.at[1], ask_recv.at[1], moved(me, "x", step), core)
    for z in (1, 3, 2):
        for x in (1, 3, 2):
            part = ask_v.at[pl.ds(slab * 8 + me["y"] * 2, 2)]
            send(part, part, ask_send.at[1], ask_recv.at[1], moved(moved(me, "z", z), "x", x), core)
    for k, (order, r0, c0, cols) in enumerate(PARTS):
        own_boxes = mult_ref.at[:, pl.ds(r0, ROWS), pl.ds(c0, cols)]
        pltpu.make_async_copy(own_boxes, boxes_of(k, me, 0, 32), g_own.at[k]).start()
    for k in range(3):
        pass_on(k)
    for k in range(3, 6):
        spread(k, 0, 16, 1, 0)
        spread(k, 16, 16, 3, 1)
        spread(k, 16, 16, 1, 2)
        spread(k, 0, 16, 3, 2)
    drain(ask_v.at[pl.ds(0, 66)], ask_recv.at[1])
    to_scalars = pltpu.make_async_copy(ask_v, ask_s, copy_sem.at[0])
    to_scalars.start()
    to_scalars.wait()

    def pack(k, steps):
        order, r0, c0, cols = PARTS[k]
        g, p, q = ORDERS[order]
        for step in steps:
            target = moved(me, p, step)

            def one(j, _):
                to = dict(target)
                to[q] = j // 8
                asker = index_of(to, (j // 4) % 2)
                source = dict(me)
                source[g] = j % 4
                served = index_of(source, core)
                for r in range(2):
                    row = ask_s[asker, r, served]
                    packed[k][target[p], 2 * j + r] = gathered[k][(j % 4) * 32 + row]
                return 0

            lax.fori_loop(0, 32, one, 0, unroll=4)
            if step:
                send(packed[k].at[target[p]], relay[k].at[me[p]], s_send.at[k], s_recv.at[k, me[p]], target, core)

    def boxes_are_here(k):
        drain(gathered[k].at[pl.ds(0, 64)], g_recv.at[k, 2])
        drain(gathered[k].at[pl.ds(0, 32)], g_own.at[k])

    def forward(k, step):
        order = PARTS[k][0]
        g, p, q = ORDERS[order]
        came = moved(me, p, step)
        src = packed[k] if step == 0 else relay[k]
        if step:
            drain(relay[k].at[came[p]], s_recv.at[k, came[p]])
        slot = ((came[p] * 4 + me[q]) * 2 + core) * 8
        for hop in (2, 1, 3, 0):
            for c in (core, 1 - core):
                to = moved(me, q, hop)
                piece = src.at[came[p], pl.ds((to[q] * 2 + c) * 8, 8)]
                dst = finals[k].at[pl.ds(slot, 8)]
                if hop == 0 and c is core:
                    pltpu.make_async_copy(piece, dst, f_own.at[k]).start()
                else:
                    send(piece, dst, f_send.at[k], f_recv.at[k], to, c)

    def near_sums():
        for way in range(2):
            drain(edge_in.at[way], edge_recv.at[way])
            drain(edge_out.at[way], edge_send.at[way])
        here = (mine > 0, mine < 127)
        for way in range(2):
            edge_in[way, 0:64, :] = jnp.where(here[way], edge_in[way, 0:64, :], 0.0)

        def half(i, before, now):
            joined = jnp.where(second, pltpu.roll(now, 64, 1), pltpu.roll(before, 64, 1))
            shifted[:, tile(i)] = joined[0:64].astype(jnp.bfloat16)
            columns[tile(i), 0:8] = jnp.transpose(joined[64:72])

        def own(i):
            return jnp.concatenate([masked(i), places[:, tile(i)]], 0)

        half(0, edge_in[0], own(0))
        half(16, own(15), edge_in[1])

        def middle(i, _):
            half(i, own(i - 1), own(i))
            return 0

        lax.fori_loop(1, 16, middle, 0)

        def pair(i, _):
            kernel_tiles = []
            for sb in range(4):
                o = jnp.where(second, sb - 2, sb - 1)
                at = columns[pl.ds(pl.multiple_of(i * 128 + sb * 64, 64), 64), 0:8]
                dx = places[0:1, tile(i)] - at[:, 0:1] - 2.0 * o.astype(jnp.float32)
                dy = places[1:2, tile(i)] - at[:, 1:2]
                dz = places[2:3, tile(i)] - at[:, 2:3]
                scaled = length_factor * jnp.sqrt(dx * dx + dy * dy + dz * dz)
                value = (1.0 + scaled) * jnp.exp(-scaled)
                kernel_tiles.append(jnp.where((o >= -1) & (o <= 1), value, 0.0))
            high, low = split(jnp.concatenate(kernel_tiles, 0))
            window = shifted[:, pl.ds(pl.multiple_of(i * 128, 128), 256)]
            potential_ref[:, tile(i)] = jnp.where(present(i), dot(window, high) + dot(window, low), 0.0)
            return 0

        lax.fori_loop(0, 16, pair, 0)

    def weight_tables():
        node = lax.broadcasted_iota(jnp.int32, (8, 128), 0)
        factors = []
        for k in range(ORDER):
            column = jnp.zeros((8, 128), jnp.float32)
            for m in range(ORDER):
                column = jnp.where(node == m, math.cos(k * (2 * m + 1) * math.pi / (2 * ORDER)), column)
            factors.append(column)

        def pair(i, _):
            weights = []
            for axis in range(3):
                u = places[axis : axis + 1, tile(i)]
                old, new = jnp.ones_like(u), u
                value = factors[0] + factors[1] * u
                for k in range(2, ORDER):
                    old, new = new, 2.0 * u * new - old
                    value = value + factors[k] * new
                weights.append((2.0 * value - 1.0) / ORDER)
            weights[2] = jnp.where(present(i), weights[2], 0.0)
            for m1 in range(ORDER):
                parts = [(weights[0][m1 : m1 + 1] * weights[1][m2 : m2 + 1]) * weights[2] for m2 in range(ORDER)]
                high, low = split(jnp.concatenate(parts, 0))
                tables[i, m1 * 64 : m1 * 64 + 64, 0:128] = high
                tables[i, m1 * 64 : m1 * 64 + 64, 128:256] = low
            return 0

        lax.fori_loop(0, 16, pair, 0)

    def load_op(t):
        return pltpu.make_async_copy(
            ops_ref.at[t], stream.at[t % 2], stream_sem.at[t % 2]
        )

    def local_type(t):
        load_op(t).wait()
        if t + 1 < 16:
            load_op(t + 1).start()

        def group(i, _):
            for b in range(8):
                lhs[b * 64 : b * 64 + 64, 0:512] = mult[local_ref[t, i * 8 + b]]
            value = dot(lhs[:, 0:512], stream[t % 2]).reshape(8, 64, 512)
            if t == 0:
                total[pl.ds(i * 8, 8)] = value
            else:
                total[pl.ds(i * 8, 8)] += value
            return 0

        lax.fori_loop(0, 4, group, 0)

    def arrived(k):
        drain(finals[k].at[pl.ds(0, 224)], f_recv.at[k])
        drain(finals[k].at[pl.ds(0, 32)], f_own.at[k])

    def remote_rows(k):
        order, r0, _, _ = PARTS[k]
        arrived(k)

        def one(half, _):
            for t in range(4):
                for b in range(32):
                    block = finals[k][slot_s[order, (4 * half + t) * 32 + b]]
                    for (_, _, c0, cols), start in zip(PARTS[3:], STARTS):
                        lhs[b * 16 : b * 16 + 16, start + t * cols : start + (t + 1) * cols] = block[:, c0 : c0 + cols]
            total[:, r0 : r0 + ROWS, :] += dot(lhs[...], ops[half]).reshape(32, ROWS, 512)
            return 0

        lax.fori_loop(0, 2, one, 0)

    def fetch(k, half, t, b):
        return finals[k][slot_s[PARTS[k][0], (4 * half + t) * 32 + b]]

    def add_last(value):
        total[:, 48:64, :] += value.reshape(32, ROWS, 512)

    def last_rows_first_part():
        arrived(3)

        def one(half, _):
            for t in range(4):
                for b in range(32):
                    lhs[b * 16 : b * 16 + 16, t * 128 : t * 128 + 128] = fetch(3, half, t, b)
            add_last(dot(lhs[:, 0:512], ops[half, 0:512]))
            return 0

        lax.fori_loop(0, 2, one, 0)

    def last_rows_other_parts():
        for k, first, cols in ((4, 0, 128), (5, 512, 256)):
            arrived(k)
            for half in range(2):
                for t in range(4):
                    at = first + t * cols
                    for b in range(32):
                        last[half, b * 16 : b * 16 + 16, at : at + cols] = fetch(k, half, t, b)

    load_op(0).start()
    for k in range(3):
        boxes_are_here(k)
        pack(k, (2,))
    for k in range(3, 6):
        pass_on(k)
    for k in range(3):
        pack(k, (1, 3, 0))
    near_sums()
    weight_tables()
    loads[0].wait()
    loads[6].wait()
    for t in range(4):
        local_type(t)
    for k in range(3, 6):
        boxes_are_here(k)
        pack(k, (1, 3, 2, 0))
    t = 4
    for ks in ((0, 1, 2), (3, 4, 5)):
        for step in (0, 2, 1, 3):
            for k in ks:
                forward(k, step)
            if t < 16:
                local_type(t)
                local_type(t + 1)
                t += 2
    drain(ops, load_sem.at[3])
    to_slots.wait()
    for k in range(3):
        remote_rows(k)
    add_far(total, 0, 48, tables, potential_ref)
    last_rows_first_part()
    last_rows_other_parts()
    for k in range(6):
        drain(finals[k].at[pl.ds(0, 224)], f_send.at[k])
        drain(packed[k].at[pl.ds(0, 3)], s_send.at[k])
        drain(gathered[k].at[pl.ds(0, 96)], g_send.at[k])
    drain(ask_v.at[pl.ds(0, 7)], ask_send.at[0])
    drain(ask_v.at[pl.ds(0, 66)], ask_send.at[1])


def finish_kernel(
    expansion_ref, potential_ref, tables, ops, last, expansion_out, potential_out, rows, potentials, sems
):
    copies = [
        pltpu.make_async_copy(
            expansion_ref.at[pl.ds(i * 8, 8), pl.ds(0, 48)], expansion_out.at[pl.ds(i * 8, 8), pl.ds(0, 48)], sems.at[i]
        )
        for i in range(4)
    ]
    copies.append(pltpu.make_async_copy(potential_ref.at[pl.ds(0, 48)], potential_out.at[pl.ds(0, 48)], sems.at[4]))
    for copy in copies:
        copy.start()
    rows[...] = expansion_ref[:, 48:64, :]

    def one(half, _):
        rows[...] += dot(last[half], ops[half, 512:2048]).reshape(32, ROWS, 512)
        return 0

    lax.fori_loop(0, 2, one, 0)
    copies.append(pltpu.make_async_copy(rows, expansion_out.at[:, pl.ds(48, 16)], sems.at[5]))
    copies[-1].start()
    potentials[...] = potential_ref[48:64, :]
    add_far(rows, 0, ROWS, tables, potentials)
    copies.append(pltpu.make_async_copy(potentials, potential_out.at[pl.ds(48, 16)], sems.at[6]))
    copies[-1].start()
    for copy in copies:
        copy.wait()


def on_device(
    multipoles, translations, local_source, remote_owner, remote_box, charges, positions, leaf_count
):
    any_space = pl.BlockSpec(memory_space=pl.ANY)
    vmem = pl.BlockSpec(memory_space=pltpu.VMEM)
    dma = pltpu.SemaphoreType.DMA
    bf16, f32, i32 = jnp.bfloat16, jnp.float32, jnp.int32
    results = pl.pallas_call(
        whole_kernel,
        out_shape=[
            pltpu.VMEM((32, 64, 512), f32),
            pltpu.VMEM((64, 2048), f32),
            pltpu.VMEM((16, 512, 256), bf16),
            pltpu.VMEM((2, 2048, 512), bf16),
            pltpu.VMEM((2, 512, 1536), bf16),
        ]
        + [jax.ShapeDtypeStruct((4, 64, ROWS, part[3]), bf16) for part in PARTS],
        in_specs=[any_space] * 8,
        out_specs=[vmem] * 5 + [any_space] * 6,
        scratch_shapes=[pltpu.VMEM((128, ROWS, part[3]), bf16) for part in PARTS]
        + [pltpu.VMEM((4, 64, ROWS, part[3]), bf16) for part in PARTS]
        + [pltpu.VMEM((256, ROWS, part[3]), bf16) for part in PARTS]
        + [
            pltpu.VMEM((128, 2, 128), i32),
            pltpu.SMEM((128, 2, 128), i32),
            pltpu.VMEM((8, 256), i32),
            pltpu.SMEM((8, 256), i32),
            pltpu.VMEM((32, 64, 512), bf16),
            pltpu.VMEM((2, 512, 512), bf16),
            pltpu.VMEM((512, 2048), bf16),
            pltpu.VMEM((64, 2048), bf16),
            pltpu.VMEM((8, 2048), f32),
            pltpu.VMEM((64, 2176), bf16),
            pltpu.VMEM((2176, 8), f32),
            pltpu.VMEM((2, 72, 128), f32),
            pltpu.VMEM((2, 72, 128), f32),
            pltpu.VMEM((2, 2, 128), i32),
            pltpu.SMEM((16, 32), i32),
            pltpu.SMEM((32,), i32),
            dma((2,)), dma((2,)), dma((2,)), dma((6,)), dma((6, 3)), dma((6,)), dma((6,)), dma((6, 4)), dma((6,)), dma((6,)), dma((6,)),
            dma((8,)), dma((2,)), dma((2,)), dma((2,)),
        ],
        compiler_params=pltpu.CompilerParams(collective_id=0, has_side_effects=True, vmem_limit_bytes=48 * 2**20),
    )(remote_owner.reshape(2, 128), remote_box.reshape(2, 128), local_source, leaf_count, multipoles, translations, charges, positions)
    held = [pltpu.with_memory_space_constraint(value, pltpu.VMEM) for value in results[:5]]
    return pl.pallas_call(
        finish_kernel,
        out_shape=[jax.ShapeDtypeStruct((32, 64, 512), f32), jax.ShapeDtypeStruct((64, 2048), f32)],
        in_specs=[vmem] * 5,
        out_specs=[any_space] * 2,
        scratch_shapes=[pltpu.VMEM((32, ROWS, 512), f32), pltpu.VMEM((ROWS, 2048), f32), dma((7,))],
        compiler_params=pltpu.CompilerParams(vmem_limit_bytes=4 * 2**20),
    )(*held)


def solution(mesh):
    placed = (
        P(("slab", "sub"), None, None),
        P(),
        P(None, ("slab", "sub")),
        P(("slab", "sub"), None),
        P(("slab", "sub")),
        P(None, ("slab", "sub")),
        P(None, ("slab", "sub")),
        P(("slab", "sub")),
    )
    return jax.shard_map(
        on_device,
        mesh=mesh,
        in_specs=placed,
        out_specs=(P(("slab", "sub"), None, None), P(None, ("slab", "sub"))),
        check_vma=False,
    )
```
